128 devices in a mesh: row: 8 (over y, x_hi), col: 16 (over z, x_lo, core).
Axes of the slice: x: 4 (x_hi: 2, x_lo: 2; x = x_hi * 2 + x_lo), y: 4, z: 4, core: 2. Of those that a mesh axis runs over, the one named last changes fastest.
Arguments:
- ancestor_inverse: float32 [24576, 24576], P('row', 'col'), may hold values from -0.0546875 to 0.0546875
- lower_panel: float32 [2, 24576, 256], P(None, ('row', 'col')), may hold values from -6 to 6
- diag_factor: float32 [2, 256, 256], replicated, may hold values from -0.09375 to 0.09375
- diag_block: float32 [2, 256, 256], replicated, may hold values from -24 to 24
- pattern: int32 [2, 384], replicated, may hold values 0 or 1
Outputs:
- panel_inverse: float32 [2, 24576, 256], P(None, ('row', 'col'))
- diag_inverse: float32 [2, 256, 256], replicated
The draws below stay inside these ranges and needn't reach their ends.
All inputs are finite; a program needn't handle non-finite values.
Results may differ from the reference program's by a relative error of at most 0.000071.
Values sent between devices are 32-bit elements; how exact they have to be, the bound alone decides.
No kernel may reach another device: no remote copies, remote signals or barrier semaphores. Data moves between devices by JAX's collectives and lax.ppermute only.
A program may use at most 128 MiB of HBM per device.

```python
import jax
import jax.numpy as jnp
from jax import lax

W = 256
A = 24576
BS = 64
NS = 2
ABLK = 384


def place_ends(result, stream_key, least, largest):
    shape = result.shape
    spot = [jax.random.randint(jax.random.fold_in(stream_key, axis), (), 0, shape[axis]) for axis in range(len(shape))]
    result = result.at[tuple(spot)].set(least)
    longest = shape.index(max(shape))
    spot[longest] = (spot[longest] + 1) % shape[longest]
    return result.at[tuple(spot)].set(largest)


def strengthened(drawn, stream_key, source, target, parts, factor):
    def block_of(position):
        return (jnp.arange(drawn.shape[position]) // (drawn.shape[position] // parts)).reshape((-1,) + (1,) * (drawn.ndim - 1 - position))

    one_side = jax.random.permutation(stream_key, parts)[block_of(target)]
    far = (block_of(target) + parts // 2) % parts
    return jnp.where((block_of(source) == one_side) | (block_of(source) == far), factor * drawn, drawn)


def levels(rng, extent, shards, smallest, largest):
    loudness, own = 1.0, jax.random.fold_in(rng, 6)
    for dim, blocks in shards:
        heights = jnp.exp(jax.random.uniform(jax.random.fold_in(own, dim), (blocks,), jnp.float32, smallest / len(shards), largest / len(shards)))
        loudness = loudness * jnp.repeat(heights, extent[dim] // blocks).reshape([-1 if axis == dim else 1 for axis in range(len(extent))])
    return loudness


def scatter_about(own_key, extent, scale, reach, cuts=(), held_as=jnp.bfloat16):
    loudness = levels(own_key, extent, cuts, -0.22, 0.18) if cuts else 1.0
    values = jax.random.normal(own_key, extent, jnp.float32) * scale * loudness
    return jnp.minimum(jnp.maximum(values, -reach), reach).astype(held_as)


def bell_draw_with(rng, extent, width, most, cuts, heavy, kind=jnp.bfloat16):
    values = width * jax.random.normal(rng, extent, jnp.float32)
    if cuts:
        values = values * levels(rng, extent, cuts, -0.22, 0.18)
    return jnp.clip(strengthened(values, jax.random.fold_in(rng, 3), *heavy), -most, most).astype(kind)


def setup_inputs(seed: int = 0) -> dict:
    splits = jax.random.split(jax.random.key(seed), 6)
    return {
        "ancestor_inverse": bell_draw_with(splits[0], (A, A), A ** -0.5, 0.0546875, ((0, 8), (1, 16)), (1, 0, 16, 2.0), jnp.float32),
        "lower_panel": scatter_about(splits[1], (NS, A, W), 1.0, 6.0, ((1, 128),), jnp.float32),
        "diag_factor": scatter_about(splits[2], (NS, W, W), (16 * W) ** -0.5, 0.09375, (), jnp.float32),
        "diag_block": scatter_about(splits[3], (NS, W, W), 4.0, 24.0, (), jnp.float32),
        "pattern": place_ends((jax.random.randint(splits[4], (NS, ABLK), 0, 2) < 1).astype(jnp.int32), jax.random.fold_in(splits[4], 1), 0, 1),
    }


def reference(ancestor_inverse, lower_panel, diag_factor, diag_block, pattern):
    highest = lax.Precision.HIGHEST
    row_mask = jnp.repeat(pattern, BS, axis=1).astype(jnp.float32)
    normed = jnp.einsum('saw,swv->sav', lower_panel, diag_factor, precision=highest) * row_mask[:, :, None]

    def single(normed_one):
        return jnp.dot(ancestor_inverse, normed_one, precision=highest, preferred_element_type=jnp.float32)

    product = lax.map(single, normed)
    panel_inverse = -product * row_mask[:, :, None]
    diag_inverse = diag_block - jnp.einsum('saw,sav->swv', normed, panel_inverse, precision=highest)
    return panel_inverse, diag_inverse
```

```python
import jax
import jax.numpy as jnp
from jax import lax
from jax.sharding import Mesh, PartitionSpec as P

BS = 64
NS = 2
HIGH = lax.Precision.HIGH
ALL = ("y", "xh", "z", "xl", "k")


def send(x, axis, size, to):
    return lax.ppermute(x, axis, [(i, to(i)) for i in range(size)])


def transpose_pairs():
    return [(8 * c + r, 16 * r + c) for r in range(8) for c in range(16)]


def tile_mask(pattern, snode, start, length):
    tiles = lax.dynamic_slice_in_dim(pattern[snode], start // BS, length // BS, 0)
    return jnp.repeat(tiles, BS).astype(jnp.float32)[:, None]


def scatter_four(x, axis):
    me = lax.axis_index(axis)
    rows = x.shape[0] // 4
    part = lambda i: lax.dynamic_slice_in_dim(x, lax.rem(i, 4) * rows, rows, 0)
    got = [send(part(me + d), axis, 4, lambda i, d=d: (i + d) % 4) for d in (1, 2, 3)]
    return part(me) + got[0] + got[1] + got[2]


def others_four(x, axis):
    return [send(x, axis, 4, lambda i, d=d: (i + d) % 4) for d in (1, 2, 3)]


def sum_four(x, axis):
    got = others_four(x, axis)
    return x + got[0] + got[1] + got[2]


def gather_four(x, axis):
    me = lax.axis_index(axis)
    one, two, three = others_four(x, axis)
    twice = jnp.concatenate([three, two, one, x, three, two, one], axis=0)
    return lax.dynamic_slice_in_dim(twice, (3 - me) * x.shape[0], 4 * x.shape[0], 0)


def swap_core(x):
    return send(x, "k", 2, lambda i: i ^ 1)


def total(x):
    k = lax.axis_index("k")
    half = x.shape[0] // 2
    mine = lax.dynamic_slice_in_dim(x, k * half, half, 0)
    theirs = lax.dynamic_slice_in_dim(x, (1 - k) * half, half, 0)
    mine = mine + swap_core(theirs)
    mine = scatter_four(mine, "y")
    mine = sum_four(mine, "z")
    mine = mine + send(mine, "xl", 2, lambda i: i ^ 1)
    mine = mine + send(mine, "xh", 2, lambda i: i ^ 1)
    mine = gather_four(mine, "y")
    other = swap_core(mine)
    low = jnp.where(k == 0, mine, other)
    high = jnp.where(k == 0, other, mine)
    return jnp.concatenate([low, high], axis=0)


def local(ancestor_inverse, lower_panel, diag_factor, diag_block, pattern):
    y, xh, z, xl, k = (lax.axis_index(a) for a in ALL)
    row, col = y * 2 + xh, z * 4 + xl * 2 + k
    piece = lower_panel.shape[1]
    cols = ancestor_inverse.shape[1]
    width = lower_panel.shape[2]
    panels, diags = [], []
    for snode in range(NS):
        one = lower_panel[snode]
        factor = diag_factor[snode]
        piece_mask = tile_mask(pattern, snode, (row * 16 + col) * piece, piece)
        normed = jnp.dot(one, factor, precision=HIGH) * piece_mask

        mine = lax.ppermute(one, ALL, transpose_pairs())
        pair = send(mine, "xh", 2, lambda i: i ^ 1)
        mine1 = send(mine, "y", 4, lambda i: i ^ 1)
        pair3 = send(pair, "y", 4, lambda i: i ^ 3)
        both = jnp.stack([mine, mine1])
        mine32 = send(both, "y", 4, lambda i: i ^ 3)
        both = jnp.stack([pair, pair3])
        pair12 = send(both, "y", 4, lambda i: i ^ 1)
        parts = jnp.stack([mine, pair, mine1, pair12[0], mine32[1], pair12[1], mine32[0], pair3])
        places = jnp.arange(8)
        order = ((places // 2) ^ y) * 2 + ((places % 2) ^ xh)
        block = parts[order].reshape(cols, width)
        x = jnp.dot(block, factor, precision=HIGH) * tile_mask(pattern, snode, col * cols, cols)

        out = jnp.dot(ancestor_inverse, x, precision=HIGH)
        out = out.reshape(4, 2, 2, piece, width)
        keep = lax.dynamic_slice_in_dim(out, k, 1, 2)[:, :, 0]
        give = lax.dynamic_slice_in_dim(out, 1 - k, 1, 2)[:, :, 0]
        summed = keep + swap_core(give)
        summed = lax.psum_scatter(summed, "z", scatter_dimension=0, tiled=False)
        keep = lax.dynamic_slice_in_dim(summed, xl, 1, 0)[0]
        give = lax.dynamic_slice_in_dim(summed, 1 - xl, 1, 0)[0]
        summed = keep + send(give, "xl", 2, lambda i: i ^ 1)
        panel = -piece_mask * summed
        panels.append(panel)
        update = lax.dot_general(normed, panel, (((0,), (0,)), ((), ())), precision=HIGH)
        diags.append(diag_block[snode] - total(update))
    return jnp.stack(panels), jnp.stack(diags)


def solution(mesh):
    fine = Mesh(mesh.devices.reshape(4, 2, 4, 2, 2), ALL)
    rows, cols = ("y", "xh"), ("z", "xl", "k")
    return jax.shard_map(
        local,
        mesh=fine,
        in_specs=(P(rows, cols), P(None, ALL, None), P(), P(), P()),
        out_specs=(P(None, ALL, None), P()),
        check_vma=False,
    )
```

```python
import jax
import jax.numpy as jnp
from jax import lax
from jax.experimental import pallas as pl
from jax.experimental.pallas import tpu as pltpu
from jax.sharding import Mesh, PartitionSpec as P

BS = 64
NS = 2
HIGH = lax.Precision.HIGH
HIGHEST = lax.Precision.HIGHEST
ALL = ("y", "xh", "z", "xl", "k")
BF = jnp.bfloat16
F32 = jnp.float32


def send(x, axis, size, to):
    return lax.ppermute(x, axis, [(i, to(i)) for i in range(size)])


def swap(x, axis):
    return send(x, axis, 2, lambda i: i ^ 1)


def transpose_pairs():
    return [(8 * c + r, 16 * r + c) for r in range(8) for c in range(16)]


def tile_mask(pattern, snode, start, length):
    tiles = lax.dynamic_slice_in_dim(pattern[snode], start // BS, length // BS, 0)
    return jnp.repeat(tiles, BS).astype(F32)[:, None]


def scatter_four(x, axis):
    me = lax.axis_index(axis)
    rows = x.shape[0] // 4
    part = lambda i: lax.dynamic_slice_in_dim(x, lax.rem(i, 4) * rows, rows, 0)
    got = [send(part(me + d), axis, 4, lambda i, d=d: (i + d) % 4) for d in (1, 2, 3)]
    return part(me) + got[0] + got[1] + got[2]


def others_four(x, axis):
    return [send(x, axis, 4, lambda i, d=d: (i + d) % 4) for d in (1, 2, 3)]


def sum_four(x, axis):
    got = others_four(x, axis)
    return x + got[0] + got[1] + got[2]


def gather_four(x, axis):
    me = lax.axis_index(axis)
    one, two, three = others_four(x, axis)
    twice = jnp.concatenate([three, two, one, x, three, two, one], axis=0)
    return lax.dynamic_slice_in_dim(twice, (3 - me) * x.shape[0], 4 * x.shape[0], 0)


def total(first, second):
    k = lax.axis_index("k")
    mine = jnp.where(k == 0, first, second) + swap(jnp.where(k == 0, second, first), "k")
    mine = scatter_four(mine, "y")
    mine = sum_four(mine, "z")
    mine = mine + swap(mine, "xl")
    mine = mine + swap(mine, "xh")
    mine = gather_four(mine, "y")
    other = swap(mine, "k")
    return jnp.where(k == 0, mine, other), jnp.where(k == 0, other, mine)


def halves(x):
    high = x.astype(BF)
    return high, (x - high.astype(F32)).astype(BF)


def dot3(a, b, dims):
    ah, al = halves(a)
    bh, bl = halves(b)
    f = lambda p, q: lax.dot_general(p, q, (dims, ((), ())), preferred_element_type=F32)
    return f(ah, bh) + (f(ah, bl) + f(al, bh))


def product_kernel(place_ref, a_ref, *refs):
    pieces, (keep_ref, give_ref, high, low) = refs[:8], refs[8:]
    piece = pieces[0].shape[0]

    @pl.when(pl.program_id(0) == 0)
    def _():
        for j in range(8):
            rows = pl.ds(pl.multiple_of(place_ref[j] * piece, BS), piece)
            xh, xl = halves(pieces[j][...])
            high[rows, :] = xh
            low[rows, :] = xl

    ah, al = halves(a_ref[...])
    f = lambda p, q: jnp.dot(p, q, preferred_element_type=F32)
    out = f(ah, high[...]) + (f(ah, low[...]) + f(al, high[...]))
    first, second = out[:piece], out[piece:]
    lower = place_ref[8] == 0
    keep_ref[0] = jnp.where(lower, first, second)
    give_ref[0] = jnp.where(lower, second, first)


def product(a, pieces, places):
    rows, cols = a.shape
    piece, width = pieces[0].shape
    blocks = rows // (2 * piece)
    whole = pl.BlockSpec((piece, width), lambda i, p: (0, 0))
    out = pl.BlockSpec((1, piece, width), lambda i, p: (i, 0, 0))
    return pl.pallas_call(
        product_kernel,
        grid_spec=pltpu.PrefetchScalarGridSpec(
            num_scalar_prefetch=1,
            grid=(blocks,),
            in_specs=[pl.BlockSpec((2 * piece, cols), lambda i, p: (i, 0))] + [whole] * 8,
            out_specs=[out, out],
            scratch_shapes=[pltpu.VMEM((cols, width), BF)] * 2,
        ),
        out_shape=[jax.ShapeDtypeStruct((blocks, piece, width), F32)] * 2,
        compiler_params=pltpu.CompilerParams(vmem_limit_bytes=40 << 20),
        cost_estimate=pl.CostEstimate(
            flops=6 * rows * cols * width, bytes_accessed=4 * (rows * cols + (rows + cols) * width), transcendentals=0
        ),
    )(places, a, *pieces)


def add_kernel(keep_ref, got_ref, x_ref, sum_ref, update_ref):
    @pl.when(pl.program_id(0) == 0)
    def _():
        update_ref[...] = jnp.zeros_like(update_ref)

    both = keep_ref[0] + got_ref[0]
    sum_ref[0] = both
    update_ref[...] += dot3(x_ref[0], both, ((0,), (0,)))


def add_and_update(keep, got, x):
    blocks, piece, width = keep.shape
    spec = pl.BlockSpec((1, piece, width), lambda i: (i, 0, 0))
    return pl.pallas_call(
        add_kernel,
        grid=(blocks,),
        in_specs=[spec] * 3,
        out_specs=[spec, pl.BlockSpec((width, width), lambda i: (0, 0))],
        out_shape=[jax.ShapeDtypeStruct(keep.shape, F32), jax.ShapeDtypeStruct((width, width), F32)],
        compiler_params=pltpu.CompilerParams(vmem_limit_bytes=16 << 20),
        cost_estimate=pl.CostEstimate(
            flops=6 * blocks * piece * width * width, bytes_accessed=16 * blocks * piece * width, transcendentals=0
        ),
    )(keep, got, x)


def gather_column(mine):
    pair = swap(mine, "xh")
    one, three = (lambda i: i ^ 1), (lambda i: i ^ 3)
    mine1 = send(mine, "y", 4, one)
    mine3 = send(mine, "y", 4, three)
    pair3 = send(pair, "y", 4, three)
    mine2 = send(mine1, "y", 4, three)
    pair1 = send(pair, "y", 4, one)
    pair2 = send(pair3, "y", 4, one)
    return [mine, pair, mine1, pair1, mine2, pair2, mine3, pair3]


def local(ancestor_inverse, lower_panel, diag_factor, diag_block, pattern):
    y, xh, z, xl, k = (lax.axis_index(a) for a in ALL)
    row, col = y * 2 + xh, z * 4 + xl * 2 + k
    piece = lower_panel.shape[1]
    start = (row * 16 + col) * piece
    masks = [tile_mask(pattern, s, start, piece) for s in range(NS)]
    normed = [jnp.dot(lower_panel[s], diag_factor[s], precision=HIGHEST) * masks[s] for s in range(NS)]
    spots = jnp.arange(8, dtype=jnp.int32)
    places = jnp.concatenate([((spots // 2) ^ y) * 2 + ((spots % 2) ^ xh), k[None]])

    near = swap(normed[1], "xl")
    pair = jnp.stack([jnp.where(xl == 0, normed[1], near), jnp.where(xl == 0, near, normed[1])])
    band = lax.all_gather(pair, "z", axis=0, tiled=True)

    panels, updates = [], []
    for snode in range(NS):
        mine = lax.ppermute(normed[snode], ALL, transpose_pairs())
        keep, give = product(ancestor_inverse, gather_column(mine), places)
        got = swap(give, "k")
        if snode == 0:
            summed = keep + got
        else:
            summed, early = add_and_update(keep, got, band)
        summed = lax.psum_scatter(summed.reshape(4, 2, *summed.shape[1:]), "z", scatter_dimension=0, tiled=False)
        kept = lax.dynamic_slice_in_dim(summed, xl, 1, 0)[0]
        given = lax.dynamic_slice_in_dim(summed, 1 - xl, 1, 0)[0]
        whole = masks[snode] * (kept + swap(given, "xl"))
        panels.append(-whole)
        if snode == 0:
            late = lax.dot_general(normed[0], whole, (((0,), (0,)), ((), ())), precision=HIGH)
    first, second = total(late, early)
    return jnp.stack(panels), jnp.stack([diag_block[0] + first, diag_block[1] + second])


def solution(mesh):
    fine = Mesh(mesh.devices.reshape(4, 2, 4, 2, 2), ALL)
    rows, cols = ("y", "xh"), ("z", "xl", "k")
    return jax.shard_map(
        local,
        mesh=fine,
        in_specs=(P(rows, cols), P(None, ALL, None), P(), P(), P()),
        out_specs=(P(None, ALL, None), P()),
        check_vma=False,
    )
```

```python
import jax
import jax.numpy as jnp
from jax import lax
from jax.experimental import pallas as pl
from jax.experimental.pallas import tpu as pltpu
from jax.sharding import Mesh, PartitionSpec as P

BS = 64
NS = 2
HIGH = lax.Precision.HIGH
HIGHEST = lax.Precision.HIGHEST
ALL = ("y", "xh", "z", "xl", "k")
BF = jnp.bfloat16
F32 = jnp.float32
LIMIT = 16


def send(x, axis, size, to):
    return lax.ppermute(x, axis, [(i, to(i)) for i in range(size)])


def swap(x, axis):
    return send(x, axis, 2, lambda i: i ^ 1)


def transpose_pairs():
    return [(8 * c + r, 16 * r + c) for r in range(8) for c in range(16)]


def tile_mask(pattern, snode, start, length):
    tiles = lax.dynamic_slice_in_dim(pattern[snode], start // BS, length // BS, 0)
    return jnp.repeat(tiles, BS).astype(F32)[:, None]


def pick(bit, x, y):
    return jnp.where(bit == 0, x, y)


def total(first, second):
    k, y = lax.axis_index("k"), lax.axis_index("y")
    mine = pick(k, first, second) + swap(pick(k, second, first), "k")
    for flip, bit in ((1, (y ^ (y >> 1)) & 1), (3, y >> 1)):
        half = mine.shape[0] // 2
        low, high = mine[:half], mine[half:]
        mine = pick(bit, low, high) + send(pick(bit, high, low), "y", 4, lambda i: i ^ flip)
    for flip in (1, 3):
        mine = mine + send(mine, "z", 4, lambda i: i ^ flip)
    mine = mine + swap(mine, "xl")
    mine = mine + swap(mine, "xh")
    for flip, bit in ((3, y >> 1), (1, (y ^ (y >> 1)) & 1)):
        other = send(mine, "y", 4, lambda i: i ^ flip)
        mine = jnp.concatenate([pick(bit, mine, other), pick(bit, other, mine)])
    other = swap(mine, "k")
    return pick(k, mine, other), pick(k, other, mine)


def halves(x):
    high = x.astype(BF)
    return high, (x - high.astype(F32)).astype(BF)


def dot3(a, b, dims):
    ah, al = halves(a)
    bh, bl = halves(b)
    f = lambda p, q: lax.dot_general(p, q, (dims, ((), ())), preferred_element_type=F32)
    return f(ah, bh) + (f(ah, bl) + f(al, bh))


def split_kernel(a_ref, high_ref, low_ref):
    high_ref[...], low_ref[...] = halves(a_ref[...])


def split(a, step):
    rows, cols = a.shape
    spec = pl.BlockSpec((step, cols), lambda i: (i, 0))
    return pl.pallas_call(
        split_kernel,
        grid=(rows // step,),
        in_specs=[spec],
        out_specs=[spec, spec],
        out_shape=[jax.ShapeDtypeStruct(a.shape, BF)] * 2,
        compiler_params=pltpu.CompilerParams(vmem_limit_bytes=24 << 20),
        cost_estimate=pl.CostEstimate(flops=4 * rows * cols, bytes_accessed=8 * rows * cols, transcendentals=0),
    )(a)


def later(xs, after):
    anywhere = pl.BlockSpec(memory_space=pl.ANY)
    return pl.pallas_call(
        lambda *refs: None,
        in_specs=[anywhere] * (len(xs) + 1),
        out_specs=[anywhere] * len(xs),
        out_shape=[jax.ShapeDtypeStruct(x.shape, x.dtype) for x in xs],
        input_output_aliases={i: i for i in range(len(xs))},
        cost_estimate=pl.CostEstimate(flops=0, bytes_accessed=0, transcendentals=0),
    )(*xs, after)


def product_kernel(place_ref, ah_ref, al_ref, *refs):
    pieces, (keep_ref, give_ref, high, low) = refs[:8], refs[-4:]
    piece = pieces[0].shape[0]

    @pl.when(pl.program_id(0) == 0)
    def _():
        for j in range(8):
            rows = pl.ds(pl.multiple_of(place_ref[j] * piece, BS), piece)
            xh, xl = halves(pieces[j][...])
            high[rows, :] = xh
            low[rows, :] = xl

    ah, al = ah_ref[...], al_ref[...]
    f = lambda p, q: jnp.dot(p, q, preferred_element_type=F32)
    out = f(ah, high[...]) + (f(ah, low[...]) + f(al, high[...]))
    first, second = out[:piece], out[piece:]
    lower = place_ref[8] == 0
    keep_ref[0] = jnp.where(lower, first, second)
    give_ref[0] = jnp.where(lower, second, first)


def product(parts, pieces, places, after=()):
    rows, cols = parts[0].shape
    piece, width = pieces[0].shape
    blocks = rows // (2 * piece)
    whole = pl.BlockSpec((piece, width), lambda i, p: (0, 0))
    out = pl.BlockSpec((1, piece, width), lambda i, p: (i, 0, 0))
    return pl.pallas_call(
        product_kernel,
        grid_spec=pltpu.PrefetchScalarGridSpec(
            num_scalar_prefetch=1,
            grid=(blocks,),
            in_specs=[pl.BlockSpec((2 * piece, cols), lambda i, p: (i, 0))] * 2
            + [whole] * 8
            + [pl.BlockSpec(memory_space=pl.ANY)] * len(after),
            out_specs=[out, out],
            scratch_shapes=[pltpu.VMEM((cols, width), BF)] * 2,
        ),
        out_shape=[jax.ShapeDtypeStruct((blocks, piece, width), F32)] * 2,
        compiler_params=pltpu.CompilerParams(vmem_limit_bytes=LIMIT << 20),
        cost_estimate=pl.CostEstimate(
            flops=6 * rows * cols * width, bytes_accessed=4 * (rows * cols + (rows + cols) * width), transcendentals=0
        ),
    )(places, *parts, *pieces, *after)


def add_kernel(block_ref, keep_ref, got_ref, x_ref, *refs):
    outs, update_ref = refs[:-1], refs[-1]
    step = pl.program_id(0)

    @pl.when(step == 0)
    def _():
        update_ref[...] = jnp.zeros_like(update_ref)

    both = keep_ref[0] + got_ref[0]
    each = pl.num_programs(0) // len(outs)
    for j, out in enumerate(outs):

        @pl.when(step // each == j)
        def _():
            out[0] = both

    update_ref[...] += dot3(x_ref[0], both, ((0,), (0,)))


def add_and_update(keep, got, x, blocks, parts):
    count, piece, width = keep.shape
    each = count // parts
    spec = pl.BlockSpec((1, piece, width), lambda i, b: (b[i], 0, 0))
    outs = [
        pl.BlockSpec((1, piece, width), lambda i, b, j=j: (jnp.clip(i - j * each, 0, each - 1), 0, 0)) for j in range(parts)
    ]
    *sums, update = pl.pallas_call(
        add_kernel,
        grid_spec=pltpu.PrefetchScalarGridSpec(
            num_scalar_prefetch=1,
            grid=(count,),
            in_specs=[spec] * 3,
            out_specs=[*outs, pl.BlockSpec((width, width), lambda i, b: (0, 0))],
        ),
        out_shape=[jax.ShapeDtypeStruct((each, piece, width), F32)] * parts + [jax.ShapeDtypeStruct((width, width), F32)],
        compiler_params=pltpu.CompilerParams(vmem_limit_bytes=16 << 20),
        cost_estimate=pl.CostEstimate(
            flops=6 * count * piece * width * width, bytes_accessed=16 * count * piece * width, transcendentals=0
        ),
    )(blocks, keep, got, x)
    return sums, update


def near_pieces(mine):
    return swap(mine, "xh"), send(mine, "y", 4, lambda i: i ^ 1), send(mine, "y", 4, lambda i: i ^ 3)


def gather_column(mine, pair, mine1, mine3):
    one, three = (lambda i: i ^ 1), (lambda i: i ^ 3)
    pair3 = send(pair, "y", 4, three)
    pair1 = send(pair, "y", 4, one)
    mine2 = send(mine1, "y", 4, three)
    pair2 = send(pair3, "y", 4, one)
    return [mine, pair, mine1, pair1, mine2, pair2, mine3, pair3]


def sum_scattered(sums, z):
    give_a, give_b, keep_a, keep_b = sums
    one, three = (lambda i: i ^ 1), (lambda i: i ^ 3)
    got_a = send(give_a, "z", 4, one)
    got_b = send(give_b, "z", 4, three)
    next_a = send(keep_a[1] + got_a[1], "z", 4, three)
    next_b = send(keep_b[1] + got_b[1], "z", 4, one)
    return (keep_a[0] + got_a[0]) + next_a, (keep_b[0] + got_b[0]) + next_b


def local(ancestor_inverse, lower_panel, diag_factor, diag_block, pattern):
    y, xh, z, xl, k = (lax.axis_index(a) for a in ALL)
    row, col = y * 2 + xh, z * 4 + xl * 2 + k
    piece = lower_panel.shape[1]
    start = (row * 16 + col) * piece
    masks = [tile_mask(pattern, s, start, piece) for s in range(NS)]
    normed = [jnp.dot(lower_panel[s], diag_factor[s], precision=HIGHEST) * masks[s] for s in range(NS)]
    spots = jnp.arange(8, dtype=jnp.int32)
    places = jnp.concatenate([((spots // 2) ^ y) * 2 + ((spots % 2) ^ xh), k[None]])

    mine = [lax.ppermute(n, ALL, transpose_pairs()) for n in normed]

    near = [swap(n, "xl") for n in normed]
    pairs = [jnp.stack([pick(xl, n, m), pick(xl, m, n)]) for n, m in zip(normed, near)]
    bands = [lax.all_gather(p, "z", axis=0, tiled=True) for p in pairs]
    apart = jnp.array([1, 2, 3, 2, 0, 3, 0, 1], jnp.int32)
    half = jnp.array([0, 0, 1, 1, 0, 0, 1, 1], jnp.int32)
    halving = (apart ^ z) * 2 + half

    parts = split(ancestor_inverse, 2 * piece)
    near = [near_pieces(m) for m in mine]
    panels, updates = [], []
    for snode in range(NS):
        if snode == 0:
            after = (mine[1], *pairs)
            around = near[0]
        else:
            after = ()
            around = later(near[1], keep)
        keep, give = product(parts, gather_column(mine[snode], *around), places, after)
        got = swap(give, "k")
        if snode == 0:
            (summed,), update = add_and_update(keep, got, bands[0], spots, 1)
            summed = lax.psum_scatter(summed.reshape(4, 2, *summed.shape[1:]), "z", scatter_dimension=0, tiled=False)
            first, second = summed[0], summed[1]
        else:
            sums, update = add_and_update(keep, got, bands[1], halving, 4)
            first, second = sum_scattered(sums, z)
        kept, given = pick(xl, first, second), pick(xl, second, first)
        panels.append(-masks[snode] * (kept + swap(given, "xl")))
        updates.append(update)
    first, second = total(*updates)
    return jnp.stack(panels), jnp.stack([diag_block[0] + first, diag_block[1] + second])


def solution(mesh):
    fine = Mesh(mesh.devices.reshape(4, 2, 4, 2, 2), ALL)
    rows, cols = ("y", "xh"), ("z", "xl", "k")
    return jax.shard_map(
        local,
        mesh=fine,
        in_specs=(P(rows, cols), P(None, ALL, None), P(), P(), P()),
        out_specs=(P(None, ALL, None), P()),
        check_vma=False,
    )
```

```python
import jax
import jax.numpy as jnp
from jax import lax
from jax.experimental import pallas as pl
from jax.experimental.pallas import tpu as pltpu
from jax.sharding import Mesh, PartitionSpec as P

BS = 64
NS = 2
HIGH = lax.Precision.HIGH
HIGHEST = lax.Precision.HIGHEST
ALL = ("y", "xh", "z", "xl", "k")
BF = jnp.bfloat16
F32 = jnp.float32


def send(x, axis, size, to):
    return lax.ppermute(x, axis, [(i, to(i)) for i in range(size)])


def swap(x, axis):
    return send(x, axis, 2, lambda i: i ^ 1)


def transpose_pairs():
    return [(8 * c + r, 16 * r + c) for r in range(8) for c in range(16)]


def tile_mask(pattern, snode, start, length):
    tiles = lax.dynamic_slice_in_dim(pattern[snode], start // BS, length // BS, 0)
    return jnp.repeat(tiles, BS).astype(F32)[:, None]


def scatter_four(x, axis):
    me = lax.axis_index(axis)
    rows = x.shape[0] // 4
    part = lambda i: lax.dynamic_slice_in_dim(x, lax.rem(i, 4) * rows, rows, 0)
    got = [send(part(me + d), axis, 4, lambda i, d=d: (i + d) % 4) for d in (1, 2, 3)]
    return part(me) + got[0] + got[1] + got[2]


def others_four(x, axis):
    return [send(x, axis, 4, lambda i, d=d: (i + d) % 4) for d in (1, 2, 3)]


def sum_four(x, axis):
    got = others_four(x, axis)
    return x + got[0] + got[1] + got[2]


def gather_four(x, axis):
    me = lax.axis_index(axis)
    one, two, three = others_four(x, axis)
    twice = jnp.concatenate([three, two, one, x, three, two, one], axis=0)
    return lax.dynamic_slice_in_dim(twice, (3 - me) * x.shape[0], 4 * x.shape[0], 0)


def total(first, second):
    k = lax.axis_index("k")
    mine = jnp.where(k == 0, first, second) + swap(jnp.where(k == 0, second, first), "k")
    mine = scatter_four(mine, "y")
    mine = sum_four(mine, "z")
    mine = mine + swap(mine, "xl")
    mine = mine + swap(mine, "xh")
    mine = gather_four(mine, "y")
    other = swap(mine, "k")
    return jnp.where(k == 0, mine, other), jnp.where(k == 0, other, mine)


def halves(x):
    high = x.astype(BF)
    return high, (x - high.astype(F32)).astype(BF)


def dot3(a, b, dims):
    ah, al = halves(a)
    bh, bl = halves(b)
    f = lambda p, q: lax.dot_general(p, q, (dims, ((), ())), preferred_element_type=F32)
    return f(ah, bh) + (f(ah, bl) + f(al, bh))


def later(xs, after):
    anywhere = pl.BlockSpec(memory_space=pl.ANY)
    return pl.pallas_call(
        lambda *refs: None,
        in_specs=[anywhere] * (len(xs) + 1),
        out_specs=[anywhere] * len(xs),
        out_shape=[jax.ShapeDtypeStruct(x.shape, x.dtype) for x in xs],
        input_output_aliases={i: i for i in range(len(xs))},
        cost_estimate=pl.CostEstimate(flops=0, bytes_accessed=0, transcendentals=0),
    )(*xs, after)


def product_kernel(place_ref, a_ref, *refs):
    pieces, (keep_ref, give_ref) = refs[:8], refs[-10:-8]
    rows_in, a_in, high, low, kept, given, sems, outs = refs[-8:]
    blocks = kept.shape[0]
    piece = kept.shape[1]

    def block_copy(i):
        return pltpu.make_async_copy(a_ref.at[pl.ds(i * 2 * piece, 2 * piece)], a_in.at[i], sems.at[8 + i])

    copies = [pltpu.make_async_copy(pieces[j], rows_in.at[j], sems.at[j]) for j in range(8)]
    for c in copies:
        c.start()
    for i in range(blocks):
        block_copy(i).start()
    for j, c in enumerate(copies):
        c.wait()
        rows = pl.ds(pl.multiple_of(place_ref[j] * piece, BS), piece)
        xh, xl = halves(rows_in[j])
        high[rows, :] = xh
        low[rows, :] = xl
    lower = place_ref[8] == 0
    f = lambda p, q: jnp.dot(p, q, preferred_element_type=F32)

    def out_copies(i):
        return (
            pltpu.make_async_copy(kept.at[i], keep_ref.at[i], outs.at[0, i]),
            pltpu.make_async_copy(given.at[i], give_ref.at[i], outs.at[1, i]),
        )

    def body(i, _):
        block_copy(i).wait()
        ah, al = halves(a_in[i])
        out = f(ah, high[...]) + (f(ah, low[...]) + f(al, high[...]))
        first, second = out[:piece], out[piece:]
        kept[i] = jnp.where(lower, first, second)
        given[i] = jnp.where(lower, second, first)
        for c in out_copies(i):
            c.start()
        return 0

    lax.fori_loop(0, blocks, body, 0)
    for i in range(blocks):
        for c in out_copies(i):
            c.wait()


def product(a, pieces, places, after=()):
    rows, cols = a.shape
    piece, width = pieces[0].shape
    blocks = rows // (2 * piece)
    anywhere = pl.BlockSpec(memory_space=pl.ANY)
    return pl.pallas_call(
        product_kernel,
        in_specs=[pl.BlockSpec(memory_space=pltpu.SMEM)] + [anywhere] * (9 + len(after)),
        out_specs=[anywhere] * 2,
        scratch_shapes=[
            pltpu.VMEM((8, piece, width), F32),
            pltpu.VMEM((blocks, 2 * piece, cols), F32),
            pltpu.VMEM((cols, width), BF),
            pltpu.VMEM((cols, width), BF),
            pltpu.VMEM((blocks, piece, width), F32),
            pltpu.VMEM((blocks, piece, width), F32),
            pltpu.SemaphoreType.DMA((8 + blocks,)),
            pltpu.SemaphoreType.DMA((2, blocks)),
        ],
        out_shape=[jax.ShapeDtypeStruct((blocks, piece, width), F32)] * 2,
        compiler_params=pltpu.CompilerParams(vmem_limit_bytes=48 << 20),
        cost_estimate=pl.CostEstimate(
            flops=6 * rows * cols * width, bytes_accessed=4 * (rows * cols + (rows + cols) * width), transcendentals=0
        ),
    )(places, a, *pieces, *after)


def add_kernel(keep_ref, got_ref, x_ref, sum_ref, update_ref):
    @pl.when(pl.program_id(0) == 0)
    def _():
        update_ref[...] = jnp.zeros_like(update_ref)

    both = keep_ref[0] + got_ref[0]
    sum_ref[0] = both
    update_ref[...] += dot3(x_ref[0], both, ((0,), (0,)))


def add_and_update(keep, got, x):
    blocks, piece, width = keep.shape
    spec = pl.BlockSpec((1, piece, width), lambda i: (i, 0, 0))
    return pl.pallas_call(
        add_kernel,
        grid=(blocks,),
        in_specs=[spec] * 3,
        out_specs=[spec, pl.BlockSpec((width, width), lambda i: (0, 0))],
        out_shape=[jax.ShapeDtypeStruct(keep.shape, F32), jax.ShapeDtypeStruct((width, width), F32)],
        compiler_params=pltpu.CompilerParams(vmem_limit_bytes=16 << 20),
        cost_estimate=pl.CostEstimate(
            flops=6 * blocks * piece * width * width, bytes_accessed=16 * blocks * piece * width, transcendentals=0
        ),
    )(keep, got, x)


def near_pieces(mine):
    return swap(mine, "xh"), send(mine, "y", 4, lambda i: i ^ 1), send(mine, "y", 4, lambda i: i ^ 3)


def gather_column(mine, pair, mine1, mine3):
    one, three = (lambda i: i ^ 1), (lambda i: i ^ 3)
    pair3 = send(pair, "y", 4, three)
    pair1 = send(pair, "y", 4, one)
    mine2 = send(mine1, "y", 4, three)
    pair2 = send(pair3, "y", 4, one)
    return [mine, pair, mine1, pair1, mine2, pair2, mine3, pair3]


def local(ancestor_inverse, lower_panel, diag_factor, diag_block, pattern):
    y, xh, z, xl, k = (lax.axis_index(a) for a in ALL)
    row, col = y * 2 + xh, z * 4 + xl * 2 + k
    piece = lower_panel.shape[1]
    start = (row * 16 + col) * piece
    masks = [tile_mask(pattern, s, start, piece) for s in range(NS)]
    normed = [jnp.dot(lower_panel[s], diag_factor[s], precision=HIGHEST) * masks[s] for s in range(NS)]
    spots = jnp.arange(8, dtype=jnp.int32)
    places = jnp.concatenate([((spots // 2) ^ y) * 2 + ((spots % 2) ^ xh), k[None]])

    near = swap(normed[1], "xl")
    pair = jnp.stack([jnp.where(xl == 0, normed[1], near), jnp.where(xl == 0, near, normed[1])])
    band = lax.all_gather(pair, "z", axis=0, tiled=True)

    mine = [lax.ppermute(n, ALL, transpose_pairs()) for n in normed]
    panels = []
    for snode in range(NS):
        near = near_pieces(mine[snode])
        if snode == 0:
            after = (mine[1],)
        else:
            near, after = later(near, keep), ()
        keep, give = product(ancestor_inverse, gather_column(mine[snode], *near), places, after)
        got = swap(give, "k")
        if snode == 0:
            summed = keep + got
        else:
            summed, early = add_and_update(keep, got, band)
        summed = lax.psum_scatter(summed.reshape(4, 2, *summed.shape[1:]), "z", scatter_dimension=0, tiled=False)
        kept = lax.dynamic_slice_in_dim(summed, xl, 1, 0)[0]
        given = lax.dynamic_slice_in_dim(summed, 1 - xl, 1, 0)[0]
        whole = masks[snode] * (kept + swap(given, "xl"))
        panels.append(-whole)
        if snode == 0:
            late = lax.dot_general(normed[0], whole, (((0,), (0,)), ((), ())), precision=HIGH)
    first, second = total(late, early)
    return jnp.stack(panels), jnp.stack([diag_block[0] + first, diag_block[1] + second])


def solution(mesh):
    fine = Mesh(mesh.devices.reshape(4, 2, 4, 2, 2), ALL)
    rows, cols = ("y", "xh"), ("z", "xl", "k")
    return jax.shard_map(
        local,
        mesh=fine,
        in_specs=(P(rows, cols), P(None, ALL, None), P(), P(), P()),
        out_specs=(P(None, ALL, None), P()),
        check_vma=False,
    )
```

```python
import jax
import jax.numpy as jnp
from jax import lax
from jax.experimental import pallas as pl
from jax.experimental.pallas import tpu as pltpu
from jax.sharding import Mesh, PartitionSpec as P

BS = 64
NS = 2
HIGH = lax.Precision.HIGH
HIGHEST = lax.Precision.HIGHEST
ALL = ("y", "xh", "z", "xl", "k")
BF = jnp.bfloat16
F32 = jnp.float32


def send(x, axis, size, to):
    return lax.ppermute(x, axis, [(i, to(i)) for i in range(size)])


def swap(x, axis):
    return send(x, axis, 2, lambda i: i ^ 1)


def transpose_pairs():
    return [(8 * c + r, 16 * r + c) for r in range(8) for c in range(16)]


def tile_mask(pattern, snode, start, length):
    tiles = lax.dynamic_slice_in_dim(pattern[snode], start // BS, length // BS, 0)
    return jnp.repeat(tiles, BS).astype(F32)[:, None]


def scatter_four(x, axis):
    me = lax.axis_index(axis)
    rows = x.shape[0] // 4
    part = lambda i: lax.dynamic_slice_in_dim(x, lax.rem(i, 4) * rows, rows, 0)
    got = [send(part(me + d), axis, 4, lambda i, d=d: (i + d) % 4) for d in (1, 2, 3)]
    return part(me) + got[0] + got[1] + got[2]


def others_four(x, axis):
    return [send(x, axis, 4, lambda i, d=d: (i + d) % 4) for d in (1, 2, 3)]


def sum_four(x, axis):
    got = others_four(x, axis)
    return x + got[0] + got[1] + got[2]


def gather_four(x, axis):
    me = lax.axis_index(axis)
    one, two, three = others_four(x, axis)
    twice = jnp.concatenate([three, two, one, x, three, two, one], axis=0)
    return lax.dynamic_slice_in_dim(twice, (3 - me) * x.shape[0], 4 * x.shape[0], 0)


def total(first, second):
    k = lax.axis_index("k")
    mine = jnp.where(k == 0, first, second) + swap(jnp.where(k == 0, second, first), "k")
    mine = scatter_four(mine, "y")
    mine = sum_four(mine, "z")
    mine = mine + swap(mine, "xl")
    mine = mine + swap(mine, "xh")
    mine = gather_four(mine, "y")
    other = swap(mine, "k")
    return jnp.where(k == 0, mine, other), jnp.where(k == 0, other, mine)


def halves(x):
    high = x.astype(BF)
    return high, (x - high.astype(F32)).astype(BF)


def dot3(a, b, dims):
    ah, al = halves(a)
    bh, bl = halves(b)
    f = lambda p, q: lax.dot_general(p, q, (dims, ((), ())), preferred_element_type=F32)
    return f(ah, bh) + (f(ah, bl) + f(al, bh))


def product_kernel(place_ref, a_ref, *refs):
    pieces, (keep_ref, give_ref, high, low) = refs[:8], refs[8:]
    piece = pieces[0].shape[0]

    @pl.when(pl.program_id(0) == 0)
    def _():
        for j in range(8):
            rows = pl.ds(pl.multiple_of(place_ref[j] * piece, BS), piece)
            xh, xl = halves(pieces[j][...])
            high[rows, :] = xh
            low[rows, :] = xl

    ah, al = halves(a_ref[...])
    f = lambda p, q: jnp.dot(p, q, preferred_element_type=F32)
    out = f(ah, high[...]) + (f(ah, low[...]) + f(al, high[...]))
    first, second = out[:piece], out[piece:]
    lower = place_ref[8] == 0
    keep_ref[0] = jnp.where(lower, first, second)
    give_ref[0] = jnp.where(lower, second, first)


def product(a, pieces, places):
    rows, cols = a.shape
    piece, width = pieces[0].shape
    blocks = rows // (2 * piece)
    whole = pl.BlockSpec((piece, width), lambda i, p: (0, 0), pipeline_mode=pl.Buffered(1))
    out = pl.BlockSpec((1, piece, width), lambda i, p: (i, 0, 0))
    return pl.pallas_call(
        product_kernel,
        grid_spec=pltpu.PrefetchScalarGridSpec(
            num_scalar_prefetch=1,
            grid=(blocks,),
            in_specs=[pl.BlockSpec((2 * piece, cols), lambda i, p: (i, 0))] + [whole] * 8,
            out_specs=[out, out],
            scratch_shapes=[pltpu.VMEM((cols, width), BF)] * 2,
        ),
        out_shape=[jax.ShapeDtypeStruct((blocks, piece, width), F32)] * 2,
        compiler_params=pltpu.CompilerParams(vmem_limit_bytes=40 << 20),
        cost_estimate=pl.CostEstimate(
            flops=6 * rows * cols * width, bytes_accessed=4 * (rows * cols + (rows + cols) * width), transcendentals=0
        ),
    )(places, a, *pieces)


def update_kernel(sum_ref, x_ref, first_ref, second_ref):
    @pl.when(pl.program_id(0) == 0)
    def _():
        first_ref[...] = jnp.zeros_like(first_ref)
        second_ref[...] = jnp.zeros_like(second_ref)

    both, x = sum_ref[0], x_ref[0]
    wide = first_ref.shape[0]
    first_ref[...] += dot3(x[:, :wide], both[:, :wide], ((0,), (0,)))
    second_ref[...] += dot3(x[:, wide:], both[:, wide:], ((0,), (0,)))


def updates(summed, x):
    blocks, piece, width = summed.shape
    wide = width // NS
    spec = pl.BlockSpec((1, piece, width), lambda i: (i, 0, 0))
    update = pl.BlockSpec((wide, wide), lambda i: (0, 0))
    return pl.pallas_call(
        update_kernel,
        grid=(blocks,),
        in_specs=[spec] * 2,
        out_specs=[update, update],
        out_shape=[jax.ShapeDtypeStruct((wide, wide), F32)] * 2,
        compiler_params=pltpu.CompilerParams(vmem_limit_bytes=16 << 20),
        cost_estimate=pl.CostEstimate(
            flops=6 * blocks * piece * width * wide, bytes_accessed=8 * blocks * piece * width, transcendentals=0
        ),
    )(summed, x)


def gather_column(mine):
    pair = swap(mine, "xh")
    one, three = (lambda i: i ^ 1), (lambda i: i ^ 3)
    mine1 = send(mine, "y", 4, one)
    mine3 = send(mine, "y", 4, three)
    pair3 = send(pair, "y", 4, three)
    mine2 = send(mine1, "y", 4, three)
    pair1 = send(pair, "y", 4, one)
    pair2 = send(pair3, "y", 4, one)
    return [mine, pair, mine1, pair1, mine2, pair2, mine3, pair3]


def local(ancestor_inverse, lower_panel, diag_factor, diag_block, pattern):
    y, xh, z, xl, k = (lax.axis_index(a) for a in ALL)
    row, col = y * 2 + xh, z * 4 + xl * 2 + k
    piece, wide = lower_panel.shape[1:]
    start = (row * 16 + col) * piece
    masks = [tile_mask(pattern, s, start, piece) for s in range(NS)]
    normed = jnp.concatenate(
        [jnp.dot(lower_panel[s], diag_factor[s], precision=HIGHEST) * masks[s] for s in range(NS)], axis=1
    )
    spots = jnp.arange(8, dtype=jnp.int32)
    places = jnp.concatenate([((spots // 2) ^ y) * 2 + ((spots % 2) ^ xh), k[None]])
    mine = lax.ppermute(normed, ALL, transpose_pairs())

    band = lax.all_gather(normed, ("z", "xl"), axis=0, tiled=False)

    keep, give = product(ancestor_inverse, gather_column(mine), places)
    got = swap(give, "k")
    summed = keep + got
    first, second = updates(summed, band)
    summed = lax.psum_scatter(summed.reshape(4, 2, *summed.shape[1:]), "z", scatter_dimension=0, tiled=False)
    kept = lax.dynamic_slice_in_dim(summed, xl, 1, 0)[0]
    given = lax.dynamic_slice_in_dim(summed, 1 - xl, 1, 0)[0]
    whole = kept + swap(given, "xl")
    panels = [-masks[s] * whole[:, s * wide : (s + 1) * wide] for s in range(NS)]
    first, second = total(first, second)
    return jnp.stack(panels), jnp.stack([diag_block[0] + first, diag_block[1] + second])


def solution(mesh):
    fine = Mesh(mesh.devices.reshape(4, 2, 4, 2, 2), ALL)
    rows, cols = ("y", "xh"), ("z", "xl", "k")
    return jax.shard_map(
        local,
        mesh=fine,
        in_specs=(P(rows, cols), P(None, ALL, None), P(), P(), P()),
        out_specs=(P(None, ALL, None), P()),
        check_vma=False,
    )
```

```python
import jax
import jax.numpy as jnp
from jax import lax
from jax.experimental import pallas as pl
from jax.experimental.pallas import tpu as pltpu
from jax.sharding import Mesh, PartitionSpec as P

BS = 64
NS = 2
HIGH = lax.Precision.HIGH
HIGHEST = lax.Precision.HIGHEST
ALL = ("y", "xh", "z", "xl", "k")
BF = jnp.bfloat16
F32 = jnp.float32


def send(x, axis, size, to):
    return lax.ppermute(x, axis, [(i, to(i)) for i in range(size)])


def swap(x, axis):
    return send(x, axis, 2, lambda i: i ^ 1)


def transpose_pairs():
    return [(8 * c + r, 16 * r + c) for r in range(8) for c in range(16)]


def tile_mask(pattern, snode, start, length):
    tiles = lax.dynamic_slice_in_dim(pattern[snode], start // BS, length // BS, 0)
    return jnp.repeat(tiles, BS).astype(F32)[:, None]


def scatter_four(x, axis):
    me = lax.axis_index(axis)
    rows = x.shape[0] // 4
    part = lambda i: lax.dynamic_slice_in_dim(x, lax.rem(i, 4) * rows, rows, 0)
    got = [send(part(me + d), axis, 4, lambda i, d=d: (i + d) % 4) for d in (1, 2, 3)]
    return part(me) + got[0] + got[1] + got[2]


def others_four(x, axis):
    return [send(x, axis, 4, lambda i, d=d: (i + d) % 4) for d in (1, 2, 3)]


def sum_four(x, axis):
    got = others_four(x, axis)
    return x + got[0] + got[1] + got[2]


def gather_four(x, axis):
    me = lax.axis_index(axis)
    one, two, three = others_four(x, axis)
    twice = jnp.concatenate([three, two, one, x, three, two, one], axis=0)
    return lax.dynamic_slice_in_dim(twice, (3 - me) * x.shape[0], 4 * x.shape[0], 0)


def total(first, second, before):
    k = lax.axis_index("k")
    mine = jnp.where(k == 0, first, second) + swap(jnp.where(k == 0, second, first), "k")
    mine = scatter_four(mine, "y")
    mine = sum_four(mine, "z")
    mine = mine + swap(mine, "xl")
    mine = mine + swap(mine, "xh")
    mine = gather_four(mine, "y")
    (mine,) = later([mine], [before])
    other = swap(mine, "k")
    return jnp.where(k == 0, mine, other), jnp.where(k == 0, other, mine)


def halves(x):
    high = x.astype(BF)
    return high, (x - high.astype(F32)).astype(BF)


def dot3(a, b, dims):
    ah, al = halves(a)
    bh, bl = halves(b)
    f = lambda p, q: lax.dot_general(p, q, (dims, ((), ())), preferred_element_type=F32)
    return f(ah, bh) + (f(ah, bl) + f(al, bh))


def later(xs, after):
    anywhere = pl.BlockSpec(memory_space=pl.ANY)
    return pl.pallas_call(
        lambda *refs: None,
        in_specs=[anywhere] * (len(xs) + len(after)),
        out_specs=[anywhere] * len(xs),
        out_shape=[jax.ShapeDtypeStruct(x.shape, x.dtype) for x in xs],
        input_output_aliases={i: i for i in range(len(xs))},
        cost_estimate=pl.CostEstimate(flops=0, bytes_accessed=0, transcendentals=0),
    )(*xs, *after)


def product_kernel(place_ref, a_ref, *refs):
    pieces, (keep_ref, give_ref, high, low) = refs[:8], refs[8:]
    piece = pieces[0].shape[0]

    @pl.when(pl.program_id(0) == 0)
    def _():
        for j in range(8):
            rows = pl.ds(pl.multiple_of(place_ref[j] * piece, BS), piece)
            xh, xl = halves(pieces[j][...])
            high[rows, :] = xh
            low[rows, :] = xl

    ah, al = halves(a_ref[...])
    f = lambda p, q: jnp.dot(p, q, preferred_element_type=F32)
    out = f(ah, high[...]) + (f(ah, low[...]) + f(al, high[...]))
    first, second = out[:piece], out[piece:]
    lower = place_ref[8] == 0
    keep_ref[0] = jnp.where(lower, first, second)
    give_ref[0] = jnp.where(lower, second, first)


def product(a, pieces, places, part):
    rows, cols = a.shape[0] // 2, a.shape[1]
    piece, width = pieces[0].shape
    blocks = rows // (2 * piece)
    whole = pl.BlockSpec((piece, width), lambda i, p: (0, 0), pipeline_mode=pl.Buffered(1))
    out = pl.BlockSpec((1, piece, width), lambda i, p: (i, 0, 0))
    return pl.pallas_call(
        product_kernel,
        grid_spec=pltpu.PrefetchScalarGridSpec(
            num_scalar_prefetch=1,
            grid=(blocks,),
            in_specs=[pl.BlockSpec((2 * piece, cols), lambda i, p: (2 * i + part, 0))] + [whole] * 8,
            out_specs=[out, out],
            scratch_shapes=[pltpu.VMEM((cols, width), BF)] * 2,
        ),
        out_shape=[jax.ShapeDtypeStruct((blocks, piece, width), F32)] * 2,
        compiler_params=pltpu.CompilerParams(vmem_limit_bytes=40 << 20),
        cost_estimate=pl.CostEstimate(
            flops=6 * rows * cols * width, bytes_accessed=4 * (rows * cols + (rows + cols) * width), transcendentals=0
        ),
    )(places, a, *pieces)


def update_kernel(near_ref, far_ref, x_ref, first_ref, second_ref):
    @pl.when(pl.program_id(0) == 0)
    def _():
        first_ref[...] = jnp.zeros_like(first_ref)
        second_ref[...] = jnp.zeros_like(second_ref)

    wide = first_ref.shape[0]
    for h, ref in enumerate((near_ref, far_ref)):
        both, x = ref[0], x_ref[h]
        first_ref[...] += dot3(x[:, :wide], both[:, :wide], ((0,), (0,)))
        second_ref[...] += dot3(x[:, wide:], both[:, wide:], ((0,), (0,)))


def updates(halved, x):
    blocks, piece, width = halved[0].shape
    wide = width // NS
    spec = pl.BlockSpec((1, piece, width), lambda i: (i, 0, 0))
    update = pl.BlockSpec((wide, wide), lambda i: (0, 0))
    return pl.pallas_call(
        update_kernel,
        grid=(blocks,),
        in_specs=[spec, spec, pl.BlockSpec((2, piece, width), lambda i: (i, 0, 0))],
        out_specs=[update, update],
        out_shape=[jax.ShapeDtypeStruct((wide, wide), F32)] * 2,
        compiler_params=pltpu.CompilerParams(vmem_limit_bytes=16 << 20),
        cost_estimate=pl.CostEstimate(
            flops=12 * blocks * piece * width * wide, bytes_accessed=16 * blocks * piece * width, transcendentals=0
        ),
    )(*halved, x)


def gather_column(mine):
    pair = swap(mine, "xh")
    one, three = (lambda i: i ^ 1), (lambda i: i ^ 3)
    mine1 = send(mine, "y", 4, one)
    mine3 = send(mine, "y", 4, three)
    pair3 = send(pair, "y", 4, three)
    mine2 = send(mine1, "y", 4, three)
    pair1 = send(pair, "y", 4, one)
    pair2 = send(pair3, "y", 4, one)
    return [mine, pair, mine1, pair1, mine2, pair2, mine3, pair3]


def local(ancestor_inverse, lower_panel, diag_factor, diag_block, pattern):
    y, xh, z, xl, k = (lax.axis_index(a) for a in ALL)
    row, col = y * 2 + xh, z * 4 + xl * 2 + k
    piece, wide = lower_panel.shape[1:]
    start = (row * 16 + col) * piece
    masks = [tile_mask(pattern, s, start, piece) for s in range(NS)]
    normed = jnp.concatenate(
        [jnp.dot(lower_panel[s], diag_factor[s], precision=HIGHEST) * masks[s] for s in range(NS)], axis=1
    )
    spots = jnp.arange(8, dtype=jnp.int32)
    places = jnp.concatenate([((spots // 2) ^ y) * 2 + ((spots % 2) ^ xh), k[None]])
    mine = lax.ppermute(normed, ALL, transpose_pairs())

    (sent,) = later([normed], [mine])
    band = lax.all_gather(sent, ("z", "xl"), axis=0, tiled=False)

    pieces = gather_column(mine)
    halved = []
    for part in range(2):
        keep, give = product(ancestor_inverse, pieces, places, part)
        halved.append(keep + swap(give, "k"))
    first, second = updates(halved, band)
    sums = [lax.psum_scatter(h, "z", scatter_dimension=0, tiled=False) for h in halved]
    given = jnp.where(xl == 0, sums[1], sums[0])
    taken = swap(given, "xl")
    whole = jnp.where(xl == 0, sums[0], sums[1]) + taken
    panels = [-masks[s] * whole[:, s * wide : (s + 1) * wide] for s in range(NS)]
    first, second = total(first, second, taken)
    return jnp.stack(panels), jnp.stack([diag_block[0] + first, diag_block[1] + second])


def solution(mesh):
    fine = Mesh(mesh.devices.reshape(4, 2, 4, 2, 2), ALL)
    rows, cols = ("y", "xh"), ("z", "xl", "k")
    return jax.shard_map(
        local,
        mesh=fine,
        in_specs=(P(rows, cols), P(None, ALL, None), P(), P(), P()),
        out_specs=(P(None, ALL, None), P()),
        check_vma=False,
    )
```

```python
import jax
import jax.numpy as jnp
from jax import lax
from jax.experimental import pallas as pl
from jax.experimental.pallas import tpu as pltpu
from jax.sharding import Mesh, PartitionSpec as P

BS = 64
NS = 2
HIGH = lax.Precision.HIGH
HIGHEST = lax.Precision.HIGHEST
ALL = ("y", "xh", "z", "xl", "k")
BF = jnp.bfloat16
F32 = jnp.float32


def send(x, axis, size, to):
    return lax.ppermute(x, axis, [(i, to(i)) for i in range(size)])


def swap(x, axis):
    return send(x, axis, 2, lambda i: i ^ 1)


def transpose_pairs():
    return [(8 * c + r, 16 * r + c) for r in range(8) for c in range(16)]


def tile_mask(pattern, snode, start, length):
    tiles = lax.dynamic_slice_in_dim(pattern[snode], start // BS, length // BS, 0)
    return jnp.repeat(tiles, BS).astype(F32)[:, None]


def scatter_four(x, axis):
    me = lax.axis_index(axis)
    rows = x.shape[0] // 4
    part = lambda i: lax.dynamic_slice_in_dim(x, lax.rem(i, 4) * rows, rows, 0)
    got = [send(part(me + d), axis, 4, lambda i, d=d: (i + d) % 4) for d in (1, 2, 3)]
    return part(me) + got[0] + got[1] + got[2]


def others_four(x, axis):
    return [send(x, axis, 4, lambda i, d=d: (i + d) % 4) for d in (1, 2, 3)]


def sum_four(x, axis):
    got = others_four(x, axis)
    return x + got[0] + got[1] + got[2]


def gather_four(x, axis):
    me = lax.axis_index(axis)
    one, two, three = others_four(x, axis)
    twice = jnp.concatenate([three, two, one, x, three, two, one], axis=0)
    return lax.dynamic_slice_in_dim(twice, (3 - me) * x.shape[0], 4 * x.shape[0], 0)


def total(first, second, before):
    k = lax.axis_index("k")
    mine = jnp.where(k == 0, first, second) + swap(jnp.where(k == 0, second, first), "k")
    mine = scatter_four(mine, "y")
    mine = sum_four(mine, "z")
    mine = mine + swap(mine, "xl")
    mine = mine + swap(mine, "xh")
    mine = gather_four(mine, "y")
    (mine,) = later([mine], [before])
    other = swap(mine, "k")
    return jnp.where(k == 0, mine, other), jnp.where(k == 0, other, mine)


def halves(x):
    high = x.astype(BF)
    return high, (x - high.astype(F32)).astype(BF)


def dot3(a, b, dims):
    ah, al = halves(a)
    bh, bl = halves(b)
    f = lambda p, q: lax.dot_general(p, q, (dims, ((), ())), preferred_element_type=F32)
    return f(ah, bh) + (f(ah, bl) + f(al, bh))


def later(xs, after):
    anywhere = pl.BlockSpec(memory_space=pl.ANY)
    return pl.pallas_call(
        lambda *refs: None,
        grid=(1,),
        in_specs=[anywhere] * len(xs) + [pl.BlockSpec((8, 128), lambda i: (0, 0)) for _ in after],
        out_specs=[anywhere] * len(xs),
        out_shape=[jax.ShapeDtypeStruct(x.shape, x.dtype) for x in xs],
        input_output_aliases={i: i for i in range(len(xs))},
        cost_estimate=pl.CostEstimate(flops=0, bytes_accessed=0, transcendentals=0),
    )(*xs, *after)


def product_kernel(place_ref, a_ref, *refs):
    pieces, (keep_ref, give_ref, high, low) = refs[:8], refs[8:]
    piece = pieces[0].shape[0]

    @pl.when(pl.program_id(0) == 0)
    def _():
        for j in range(8):
            rows = pl.ds(pl.multiple_of(place_ref[j] * piece, BS), piece)
            xh, xl = halves(pieces[j][...])
            high[rows, :] = xh
            low[rows, :] = xl

    ah, al = halves(a_ref[...])
    f = lambda p, q: jnp.dot(p, q, preferred_element_type=F32)
    out = f(ah, high[...]) + (f(ah, low[...]) + f(al, high[...]))
    first, second = out[:piece], out[piece:]
    lower = place_ref[8] == 0
    keep_ref[0] = jnp.where(lower, first, second)
    give_ref[0] = jnp.where(lower, second, first)


def product(a, pieces, places):
    rows, cols = a.shape
    piece, width = pieces[0].shape
    blocks = rows // (2 * piece)
    whole = pl.BlockSpec((piece, width), lambda i, p: (0, 0), pipeline_mode=pl.Buffered(1))
    out = pl.BlockSpec((1, piece, width), lambda i, p: (i, 0, 0))
    return pl.pallas_call(
        product_kernel,
        grid_spec=pltpu.PrefetchScalarGridSpec(
            num_scalar_prefetch=1,
            grid=(blocks,),
            in_specs=[pl.BlockSpec((2 * piece, cols), lambda i, p: (i, 0))] + [whole] * 8,
            out_specs=[out, out],
            scratch_shapes=[pltpu.VMEM((cols, width), BF)] * 2,
        ),
        out_shape=[jax.ShapeDtypeStruct((blocks, piece, width), F32)] * 2,
        compiler_params=pltpu.CompilerParams(vmem_limit_bytes=40 << 20),
        cost_estimate=pl.CostEstimate(
            flops=6 * rows * cols * width, bytes_accessed=4 * (rows * cols + (rows + cols) * width), transcendentals=0
        ),
    )(places, a, *pieces)


def update_kernel(sum_ref, x_ref, first_ref, second_ref):
    @pl.when(pl.program_id(0) == 0)
    def _():
        first_ref[...] = jnp.zeros_like(first_ref)
        second_ref[...] = jnp.zeros_like(second_ref)

    both, x = sum_ref[0], x_ref[0]
    wide = first_ref.shape[0]
    first_ref[...] += dot3(x[:, :wide], both[:, :wide], ((0,), (0,)))
    second_ref[...] += dot3(x[:, wide:], both[:, wide:], ((0,), (0,)))


def updates(summed, x):
    blocks, piece, width = summed.shape
    wide = width // NS
    spec = pl.BlockSpec((1, piece, width), lambda i: (i, 0, 0))
    update = pl.BlockSpec((wide, wide), lambda i: (0, 0))
    return pl.pallas_call(
        update_kernel,
        grid=(blocks,),
        in_specs=[spec] * 2,
        out_specs=[update, update],
        out_shape=[jax.ShapeDtypeStruct((wide, wide), F32)] * 2,
        compiler_params=pltpu.CompilerParams(vmem_limit_bytes=16 << 20),
        cost_estimate=pl.CostEstimate(
            flops=6 * blocks * piece * width * wide, bytes_accessed=8 * blocks * piece * width, transcendentals=0
        ),
    )(summed, x)


def gather_column(mine):
    one, three = (lambda i: i ^ 1), (lambda i: i ^ 3)
    mine1 = send(mine, "y", 4, one)
    mine3 = send(mine, "y", 4, three)
    (pair,) = later([swap(mine, "xh")], [mine1, mine3])
    pair3 = send(pair, "y", 4, three)
    pair1 = send(pair, "y", 4, one)
    pair3, mine1 = later([pair3, mine1], [pair1])
    mine2 = send(mine1, "y", 4, three)
    pair2 = send(pair3, "y", 4, one)
    return [mine, pair, mine1, pair1, mine2, pair2, mine3, pair3]


def local(ancestor_inverse, lower_panel, diag_factor, diag_block, pattern):
    y, xh, z, xl, k = (lax.axis_index(a) for a in ALL)
    row, col = y * 2 + xh, z * 4 + xl * 2 + k
    piece, wide = lower_panel.shape[1:]
    start = (row * 16 + col) * piece
    masks = [tile_mask(pattern, s, start, piece) for s in range(NS)]
    normed = jnp.concatenate(
        [jnp.dot(lower_panel[s], diag_factor[s], precision=HIGHEST) * masks[s] for s in range(NS)], axis=1
    )
    spots = jnp.arange(8, dtype=jnp.int32)
    places = jnp.concatenate([((spots // 2) ^ y) * 2 + ((spots % 2) ^ xh), k[None]])
    mine = lax.ppermute(normed, ALL, transpose_pairs())

    band = lax.all_gather(normed, ("z", "xl"), axis=0, tiled=False)

    keep, give = product(ancestor_inverse, gather_column(mine), places)
    got = swap(give, "k")
    summed = keep + got
    first, second = updates(summed, band)
    summed = lax.psum_scatter(summed.reshape(4, 2, *summed.shape[1:]), "z", scatter_dimension=0, tiled=False)
    kept = lax.dynamic_slice_in_dim(summed, xl, 1, 0)[0]
    given = lax.dynamic_slice_in_dim(summed, 1 - xl, 1, 0)[0]
    taken = swap(given, "xl")
    whole = kept + taken
    panels = [-masks[s] * whole[:, s * wide : (s + 1) * wide] for s in range(NS)]
    first, second = total(first, second, taken)
    return jnp.stack(panels), jnp.stack([diag_block[0] + first, diag_block[1] + second])


def solution(mesh):
    fine = Mesh(mesh.devices.reshape(4, 2, 4, 2, 2), ALL)
    rows, cols = ("y", "xh"), ("z", "xl", "k")
    return jax.shard_map(
        local,
        mesh=fine,
        in_specs=(P(rows, cols), P(None, ALL, None), P(), P(), P()),
        out_specs=(P(None, ALL, None), P()),
        check_vma=False,
    )
```

```python
import functools

import jax
import jax.numpy as jnp
from jax import lax
from jax.experimental import pallas as pl
from jax.experimental.pallas import tpu as pltpu
from jax.sharding import Mesh, PartitionSpec as P

BS = 64
NS = 2
HIGH = lax.Precision.HIGH
HIGHEST = lax.Precision.HIGHEST
ALL = ("y", "xh", "z", "xl", "k")
BF = jnp.bfloat16
F32 = jnp.float32


def send(x, axis, size, to):
    return lax.ppermute(x, axis, [(i, to(i)) for i in range(size)])


def swap(x, axis):
    return send(x, axis, 2, lambda i: i ^ 1)


def transpose_pairs():
    return [(8 * c + r, 16 * r + c) for r in range(8) for c in range(16)]


def tile_mask(pattern, snode, start, length):
    tiles = lax.dynamic_slice_in_dim(pattern[snode], start // BS, length // BS, 0)
    return jnp.repeat(tiles, BS).astype(F32)[:, None]


def scatter_four(x, axis):
    me = lax.axis_index(axis)
    rows = x.shape[0] // 4
    part = lambda i: lax.dynamic_slice_in_dim(x, lax.rem(i, 4) * rows, rows, 0)
    got = [send(part(me + d), axis, 4, lambda i, d=d: (i + d) % 4) for d in (1, 2, 3)]
    return part(me) + got[0] + got[1] + got[2]


def others_four(x, axis):
    return [send(x, axis, 4, lambda i, d=d: (i + d) % 4) for d in (1, 2, 3)]


def sum_four(x, axis):
    got = others_four(x, axis)
    return x + got[0] + got[1] + got[2]


def gather_four(x, axis):
    me = lax.axis_index(axis)
    one, two, three = others_four(x, axis)
    twice = jnp.concatenate([three, two, one, x, three, two, one], axis=0)
    return lax.dynamic_slice_in_dim(twice, (3 - me) * x.shape[0], 4 * x.shape[0], 0)


def total(first, second, given, taken):
    k = lax.axis_index("k")
    mine = jnp.where(k == 0, first, second) + swap(jnp.where(k == 0, second, first), "k")
    mine = scatter_four(mine, "y")
    mine = sum_four(mine, "z")
    mine = mine + swap(mine, "xl")
    mine = mine + swap(mine, "xh")
    (mine,) = later([mine], [given])
    mine = gather_four(mine, "y")
    (mine,) = later([mine], [taken])
    other = swap(mine, "k")
    return jnp.where(k == 0, mine, other), jnp.where(k == 0, other, mine)


def halves(x):
    high = x.astype(BF)
    return high, (x - high.astype(F32)).astype(BF)


def dot3(a, b, dims):
    ah, al = halves(a)
    bh, bl = halves(b)
    f = lambda p, q: lax.dot_general(p, q, (dims, ((), ())), preferred_element_type=F32)
    return f(ah, bh) + (f(ah, bl) + f(al, bh))


def later(xs, after):
    anywhere = pl.BlockSpec(memory_space=pl.ANY)
    return pl.pallas_call(
        lambda *refs: None,
        in_specs=[anywhere] * (len(xs) + len(after)),
        out_specs=[anywhere] * len(xs),
        out_shape=[jax.ShapeDtypeStruct(x.shape, x.dtype) for x in xs],
        input_output_aliases={i: i for i in range(len(xs))},
        cost_estimate=pl.CostEstimate(flops=0, bytes_accessed=0, transcendentals=0),
    )(*xs, *after)


def product_kernel(place_ref, *refs, count, adds):
    strips, pieces = refs[: count // 2], refs[count // 2 : count // 2 + count]
    before = refs[count // 2 + count : -4]
    keep_ref, give_ref, high, low = refs[-4:]
    piece = pieces[0].shape[0]

    @pl.when(pl.program_id(0) == 0)
    def _():
        for j in range(count):
            rows = pl.ds(pl.multiple_of((j // 2) * 2 * piece + place_ref[5 + j % 2] * piece, BS), piece)
            xh, xl = halves(pieces[j][...])
            high[rows, :] = xh
            low[rows, :] = xl

    f = lambda p, q: jnp.dot(p, q, preferred_element_type=F32)
    out = None
    for m, strip in enumerate(strips):
        rows = slice(m * 2 * piece, (m + 1) * 2 * piece)
        ah, al = halves(strip[...])
        term = f(ah, high[rows, :]) + (f(ah, low[rows, :]) + f(al, high[rows, :]))
        out = term if out is None else out + term
    first, second = out[:piece], out[piece:]
    lower = place_ref[4] == 0
    kept, given = jnp.where(lower, first, second), jnp.where(lower, second, first)
    if adds:
        kept, given = kept + before[0][0], given + before[1][0]
    keep_ref[0] = kept
    give_ref[0] = given


def product(a, pieces, places, start, before=()):
    rows = a.shape[0]
    piece, width = pieces[0].shape
    count = len(pieces)
    blocks = rows // (2 * piece)
    whole = pl.BlockSpec((piece, width), lambda i, p: (0, 0), pipeline_mode=pl.Buffered(1))
    strips = [pl.BlockSpec((2 * piece, 2 * piece), lambda i, p, m=m: (i, p[start + m])) for m in range(count // 2)]
    out = pl.BlockSpec((1, piece, width), lambda i, p: (i, 0, 0))
    return pl.pallas_call(
        functools.partial(product_kernel, count=count, adds=bool(before)),
        grid_spec=pltpu.PrefetchScalarGridSpec(
            num_scalar_prefetch=1,
            grid=(blocks,),
            in_specs=[*strips] + [whole] * count + [out] * len(before),
            out_specs=[out, out],
            scratch_shapes=[pltpu.VMEM((count * piece, width), BF)] * 2,
        ),
        out_shape=[jax.ShapeDtypeStruct((blocks, piece, width), F32)] * 2,
        compiler_params=pltpu.CompilerParams(vmem_limit_bytes=40 << 20),
        cost_estimate=pl.CostEstimate(
            flops=6 * rows * count * piece * width,
            bytes_accessed=4 * (rows * count * piece + (rows + count * piece) * width),
            transcendentals=0,
        ),
    )(places, *[a] * len(strips), *pieces, *before)


def update_kernel(sum_ref, x_ref, first_ref, second_ref):
    @pl.when(pl.program_id(0) == 0)
    def _():
        first_ref[...] = jnp.zeros_like(first_ref)
        second_ref[...] = jnp.zeros_like(second_ref)

    both, x = sum_ref[0], x_ref[0]
    wide = first_ref.shape[0]
    first_ref[...] += dot3(x[:, :wide], both[:, :wide], ((0,), (0,)))
    second_ref[...] += dot3(x[:, wide:], both[:, wide:], ((0,), (0,)))


def updates(summed, x):
    blocks, piece, width = summed.shape
    wide = width // NS
    spec = pl.BlockSpec((1, piece, width), lambda i: (i, 0, 0))
    update = pl.BlockSpec((wide, wide), lambda i: (0, 0))
    return pl.pallas_call(
        update_kernel,
        grid=(blocks,),
        in_specs=[spec] * 2,
        out_specs=[update, update],
        out_shape=[jax.ShapeDtypeStruct((wide, wide), F32)] * 2,
        compiler_params=pltpu.CompilerParams(vmem_limit_bytes=16 << 20),
        cost_estimate=pl.CostEstimate(
            flops=6 * blocks * piece * width * wide, bytes_accessed=8 * blocks * piece * width, transcendentals=0
        ),
    )(summed, x)


def gather_column(mine):
    pair = swap(mine, "xh")
    one, three = (lambda i: i ^ 1), (lambda i: i ^ 3)
    mine1 = send(mine, "y", 4, one)
    mine3 = send(mine, "y", 4, three)
    pair3 = send(pair, "y", 4, three)
    mine2 = send(mine1, "y", 4, three)
    pair1 = send(pair, "y", 4, one)
    pair2 = send(pair3, "y", 4, one)
    return [mine, pair, mine1, pair1, mine2, pair2, mine3, pair3]


def local(ancestor_inverse, lower_panel, diag_factor, diag_block, pattern):
    y, xh, z, xl, k = (lax.axis_index(a) for a in ALL)
    row, col = y * 2 + xh, z * 4 + xl * 2 + k
    piece, wide = lower_panel.shape[1:]
    start = (row * 16 + col) * piece
    masks = [tile_mask(pattern, s, start, piece) for s in range(NS)]
    normed = jnp.concatenate(
        [jnp.dot(lower_panel[s], diag_factor[s], precision=HIGHEST) * masks[s] for s in range(NS)], axis=1
    )
    spots = jnp.arange(4, dtype=jnp.int32)
    places = jnp.concatenate([spots ^ y, jnp.stack([k, xh, 1 - xh])]).astype(jnp.int32)
    mine = lax.ppermute(normed, ALL, transpose_pairs())

    band = lax.all_gather(normed, ("z", "xl"), axis=0, tiled=False)

    pieces = gather_column(mine)
    keep, give = product(ancestor_inverse, pieces[:4], places, 0)
    keep, give = product(ancestor_inverse, pieces[4:], places, 2, (keep, give))
    got = swap(give, "k")
    summed = keep + got
    first, second = updates(summed, band)
    summed = lax.psum_scatter(summed.reshape(4, 2, *summed.shape[1:]), "z", scatter_dimension=0, tiled=False)
    kept = lax.dynamic_slice_in_dim(summed, xl, 1, 0)[0]
    given = lax.dynamic_slice_in_dim(summed, 1 - xl, 1, 0)[0]
    taken = swap(given, "xl")
    whole = kept + taken
    panels = [-masks[s] * whole[:, s * wide : (s + 1) * wide] for s in range(NS)]
    first, second = total(first, second, given, taken)
    return jnp.stack(panels), jnp.stack([diag_block[0] + first, diag_block[1] + second])


def solution(mesh):
    fine = Mesh(mesh.devices.reshape(4, 2, 4, 2, 2), ALL)
    rows, cols = ("y", "xh"), ("z", "xl", "k")
    return jax.shard_map(
        local,
        mesh=fine,
        in_specs=(P(rows, cols), P(None, ALL, None), P(), P(), P()),
        out_specs=(P(None, ALL, None), P()),
        check_vma=False,
    )
```

```python
import jax
import jax.numpy as jnp
from jax import lax
from jax.experimental import pallas as pl
from jax.experimental.pallas import tpu as pltpu
from jax.sharding import Mesh, PartitionSpec as P

BS = 64
NS = 2
HIGH = lax.Precision.HIGH
HIGHEST = lax.Precision.HIGHEST
ALL = ("y", "xh", "z", "xl", "k")
BF = jnp.bfloat16
F32 = jnp.float32


def send(x, axis, size, to):
    return lax.ppermute(x, axis, [(i, to(i)) for i in range(size)])


def swap(x, axis):
    return send(x, axis, 2, lambda i: i ^ 1)


def transpose_pairs():
    return [(8 * c + r, 16 * r + c) for r in range(8) for c in range(16)]


def tile_mask(pattern, snode, start, length):
    tiles = lax.dynamic_slice_in_dim(pattern[snode], start // BS, length // BS, 0)
    return jnp.repeat(tiles, BS).astype(F32)[:, None]


def scatter_four(x, axis):
    me = lax.axis_index(axis)
    rows = x.shape[0] // 4
    part = lambda i: lax.dynamic_slice_in_dim(x, lax.rem(i, 4) * rows, rows, 0)
    got = [send(part(me + d), axis, 4, lambda i, d=d: (i + d) % 4) for d in (1, 2, 3)]
    return part(me) + got[0] + got[1] + got[2]


def others_four(x, axis):
    return [send(x, axis, 4, lambda i, d=d: (i + d) % 4) for d in (1, 2, 3)]


def sum_four(x, axis):
    got = others_four(x, axis)
    return x + got[0] + got[1] + got[2]


def gather_four(x, axis):
    me = lax.axis_index(axis)
    one, two, three = others_four(x, axis)
    twice = jnp.concatenate([three, two, one, x, three, two, one], axis=0)
    return lax.dynamic_slice_in_dim(twice, (3 - me) * x.shape[0], 4 * x.shape[0], 0)


def total(first, second, given, taken):
    k = lax.axis_index("k")
    mine = jnp.where(k == 0, first, second) + swap(jnp.where(k == 0, second, first), "k")
    mine = scatter_four(mine, "y")
    mine = sum_four(mine, "z")
    mine = mine + swap(mine, "xl")
    mine = mine + swap(mine, "xh")
    (mine,) = later([mine], [given])
    mine = gather_four(mine, "y")
    (mine,) = later([mine], [taken])
    other = swap(mine, "k")
    return jnp.where(k == 0, mine, other), jnp.where(k == 0, other, mine)


def halves(x):
    high = x.astype(BF)
    return high, (x - high.astype(F32)).astype(BF)


def dot3(a, b, dims):
    ah, al = halves(a)
    bh, bl = halves(b)
    f = lambda p, q: lax.dot_general(p, q, (dims, ((), ())), preferred_element_type=F32)
    return f(ah, bh) + (f(ah, bl) + f(al, bh))


def later(xs, after):
    anywhere = pl.BlockSpec(memory_space=pl.ANY)
    return pl.pallas_call(
        lambda *refs: None,
        grid=(1,),
        in_specs=[anywhere] * len(xs) + [pl.BlockSpec((8, 128), lambda i: (0, 0))] * len(after),
        out_specs=[anywhere] * len(xs),
        out_shape=[jax.ShapeDtypeStruct(x.shape, x.dtype) for x in xs],
        input_output_aliases={i: i for i in range(len(xs))},
        cost_estimate=pl.CostEstimate(flops=0, bytes_accessed=0, transcendentals=0),
    )(*xs, *after)


def product_kernel(place_ref, a_ref, *refs):
    pieces, (out_ref, high, low) = refs[:8], refs[-3:]
    piece = pieces[0].shape[0]

    @pl.when(pl.program_id(0) == 0)
    def _():
        for j in range(8):
            rows = pl.ds(pl.multiple_of(place_ref[j] * piece, BS), piece)
            xh, xl = halves(pieces[j][...])
            high[rows, :] = xh
            low[rows, :] = xl

    ah, al = halves(a_ref[...])
    f = lambda p, q: jnp.dot(p, q, preferred_element_type=F32)
    out_ref[0] = f(ah, high[...]) + (f(ah, low[...]) + f(al, high[...]))


def product(a, pieces, places, core, after=()):
    rows, cols = a.shape
    piece, width = pieces[0].shape
    blocks = rows // (2 * piece)
    whole = pl.BlockSpec((piece, width), lambda i, p: (0, 0), pipeline_mode=pl.Buffered(1))
    return pl.pallas_call(
        product_kernel,
        grid_spec=pltpu.PrefetchScalarGridSpec(
            num_scalar_prefetch=1,
            grid=(blocks,),
            in_specs=[pl.BlockSpec((piece, cols), lambda i, p: (2 * i + p[core], 0))]
            + [whole] * 8
            + [pl.BlockSpec((1, 8, 128), lambda i, p: (0, 0, 0))] * len(after),
            out_specs=pl.BlockSpec((1, piece, width), lambda i, p: (i, 0, 0)),
            scratch_shapes=[pltpu.VMEM((cols, width), BF)] * 2,
        ),
        out_shape=jax.ShapeDtypeStruct((blocks, piece, width), F32),
        compiler_params=pltpu.CompilerParams(vmem_limit_bytes=40 << 20),
        cost_estimate=pl.CostEstimate(
            flops=3 * rows * cols * width, bytes_accessed=2 * (rows * cols + (rows + cols) * width), transcendentals=0
        ),
    )(places, a, *pieces, *after)


def update_kernel(sum_ref, x_ref, first_ref, second_ref):
    @pl.when(pl.program_id(0) == 0)
    def _():
        first_ref[...] = jnp.zeros_like(first_ref)
        second_ref[...] = jnp.zeros_like(second_ref)

    both, x = sum_ref[0], x_ref[0]
    wide = first_ref.shape[0]
    first_ref[...] += dot3(x[:, :wide], both[:, :wide], ((0,), (0,)))
    second_ref[...] += dot3(x[:, wide:], both[:, wide:], ((0,), (0,)))


def updates(summed, x):
    blocks, piece, width = summed.shape
    wide = width // NS
    spec = pl.BlockSpec((1, piece, width), lambda i: (i, 0, 0))
    update = pl.BlockSpec((wide, wide), lambda i: (0, 0))
    return pl.pallas_call(
        update_kernel,
        grid=(blocks,),
        in_specs=[spec] * 2,
        out_specs=[update, update],
        out_shape=[jax.ShapeDtypeStruct((wide, wide), F32)] * 2,
        compiler_params=pltpu.CompilerParams(vmem_limit_bytes=16 << 20),
        cost_estimate=pl.CostEstimate(
            flops=6 * blocks * piece * width * wide, bytes_accessed=8 * blocks * piece * width, transcendentals=0
        ),
    )(summed, x)


def gather_column(mine):
    pair = swap(mine, "xh")
    one, three = (lambda i: i ^ 1), (lambda i: i ^ 3)
    mine1 = send(mine, "y", 4, one)
    mine3 = send(mine, "y", 4, three)
    pair3 = send(pair, "y", 4, three)
    mine2 = send(mine1, "y", 4, three)
    pair1 = send(pair, "y", 4, one)
    pair2 = send(pair3, "y", 4, one)
    return [mine, pair, mine1, pair1, mine2, pair2, mine3, pair3]


def local(ancestor_inverse, lower_panel, diag_factor, diag_block, pattern):
    y, xh, z, xl, k = (lax.axis_index(a) for a in ALL)
    row, col = y * 2 + xh, z * 4 + xl * 2 + k
    piece, wide = lower_panel.shape[1:]
    start = (row * 16 + col) * piece
    masks = [tile_mask(pattern, s, start, piece) for s in range(NS)]
    normed = jnp.concatenate(
        [jnp.dot(lower_panel[s], diag_factor[s], precision=HIGHEST) * masks[s] for s in range(NS)], axis=1
    )
    spots = jnp.arange(8, dtype=jnp.int32)
    places = jnp.concatenate([((spots // 2) ^ y) * 2 + ((spots % 2) ^ xh), jnp.stack([k, 1 - k])]).astype(jnp.int32)
    mine = lax.ppermute(normed, ALL, transpose_pairs())

    (sent,) = later([normed], [mine])
    band = lax.all_gather(sent, ("z", "xl"), axis=0, tiled=False)

    pieces = gather_column(mine)
    give = product(ancestor_inverse, pieces, places, 9)
    got = swap(give, "k")
    keep = product(ancestor_inverse, pieces, places, 8, (give,))
    summed = keep + got
    first, second = updates(summed, band)
    summed = lax.psum_scatter(summed.reshape(4, 2, *summed.shape[1:]), "z", scatter_dimension=0, tiled=False)
    kept = lax.dynamic_slice_in_dim(summed, xl, 1, 0)[0]
    given = lax.dynamic_slice_in_dim(summed, 1 - xl, 1, 0)[0]
    taken = swap(given, "xl")
    whole = kept + taken
    panels = [-masks[s] * whole[:, s * wide : (s + 1) * wide] for s in range(NS)]
    first, second = total(first, second, given, taken)
    return jnp.stack(panels), jnp.stack([diag_block[0] + first, diag_block[1] + second])


def solution(mesh):
    fine = Mesh(mesh.devices.reshape(4, 2, 4, 2, 2), ALL)
    rows, cols = ("y", "xh"), ("z", "xl", "k")
    return jax.shard_map(
        local,
        mesh=fine,
        in_specs=(P(rows, cols), P(None, ALL, None), P(), P(), P()),
        out_specs=(P(None, ALL, None), P()),
        check_vma=False,
    )
```

```python
import functools

import jax
import jax.numpy as jnp
from jax import lax
from jax.experimental import pallas as pl
from jax.experimental.pallas import tpu as pltpu
from jax.sharding import Mesh, PartitionSpec as P

BS = 64
CUT = 2
PARTS = ((0,), (1,))
NS = 2
HIGH = lax.Precision.HIGH
HIGHEST = lax.Precision.HIGHEST
ALL = ("y", "xh", "z", "xl", "k")
BF = jnp.bfloat16
F32 = jnp.float32


def send(x, axis, size, to):
    return lax.ppermute(x, axis, [(i, to(i)) for i in range(size)])


def swap(x, axis):
    return send(x, axis, 2, lambda i: i ^ 1)


def transpose_pairs():
    return [(8 * c + r, 16 * r + c) for r in range(8) for c in range(16)]


def tile_mask(pattern, snode, start, length):
    tiles = lax.dynamic_slice_in_dim(pattern[snode], start // BS, length // BS, 0)
    return jnp.repeat(tiles, BS).astype(F32)[:, None]


def scatter_four(x, axis):
    me = lax.axis_index(axis)
    rows = x.shape[0] // 4
    part = lambda i: lax.dynamic_slice_in_dim(x, lax.rem(i, 4) * rows, rows, 0)
    got = [send(part(me + d), axis, 4, lambda i, d=d: (i + d) % 4) for d in (1, 2, 3)]
    return part(me) + got[0] + got[1] + got[2]


def others_four(x, axis):
    return [send(x, axis, 4, lambda i, d=d: (i + d) % 4) for d in (1, 2, 3)]


def sum_four(x, axis):
    got = others_four(x, axis)
    return x + got[0] + got[1] + got[2]


def gather_four(x, axis):
    me = lax.axis_index(axis)
    one, two, three = others_four(x, axis)
    twice = jnp.concatenate([three, two, one, x, three, two, one], axis=0)
    return lax.dynamic_slice_in_dim(twice, (3 - me) * x.shape[0], 4 * x.shape[0], 0)


def total(first, second, before):
    k = lax.axis_index("k")
    mine = jnp.where(k == 0, first, second) + swap(jnp.where(k == 0, second, first), "k")
    mine = scatter_four(mine, "y")
    mine = sum_four(mine, "z")
    mine = mine + swap(mine, "xl")
    mine = mine + swap(mine, "xh")
    mine = gather_four(mine, "y")
    (mine,) = later([mine], [before])
    other = swap(mine, "k")
    return jnp.where(k == 0, mine, other), jnp.where(k == 0, other, mine)


def halves(x):
    high = x.astype(BF)
    return high, (x - high.astype(F32)).astype(BF)


def dot3(a, b, dims):
    ah, al = halves(a)
    bh, bl = halves(b)
    f = lambda p, q: lax.dot_general(p, q, (dims, ((), ())), preferred_element_type=F32)
    return f(ah, bh) + (f(ah, bl) + f(al, bh))


def later(xs, after):
    anywhere = pl.BlockSpec(memory_space=pl.ANY)
    return pl.pallas_call(
        lambda *refs: None,
        grid=(1,),
        in_specs=[anywhere] * len(xs) + [pl.BlockSpec((8, 128), lambda i: (0, 0))] * len(after),
        out_specs=[anywhere] * len(xs),
        out_shape=[jax.ShapeDtypeStruct(x.shape, x.dtype) for x in xs],
        input_output_aliases={i: i for i in range(len(xs))},
        cost_estimate=pl.CostEstimate(flops=0, bytes_accessed=0, transcendentals=0),
    )(*xs, *after)


def product_kernel(place_ref, *refs, count):
    strips, pieces = refs[:count], refs[count : count + 8]
    keep_ref, give_ref, high, low = refs[-4:]
    piece = pieces[0].shape[0]

    @pl.when(pl.program_id(0) == 0)
    def _():
        for j in range(8):
            rows = pl.ds(pl.multiple_of(place_ref[j] * piece, BS), piece)
            xh, xl = halves(pieces[j][...])
            high[rows, :] = xh
            low[rows, :] = xl

    ah, al = halves(jnp.concatenate([strip[...] for strip in strips], axis=0))
    f = lambda p, q: jnp.dot(p, q, preferred_element_type=F32)
    out = f(ah, high[...]) + (f(ah, low[...]) + f(al, high[...]))
    some = out.shape[0] // 2
    first, second = out[:some], out[some:]
    lower = place_ref[8] == 0
    keep_ref[0] = jnp.where(lower, first, second)
    give_ref[0] = jnp.where(lower, second, first)


def product(a, pieces, places, part, after):
    rows, cols = a.shape
    piece, width = pieces[0].shape
    blocks = rows // (2 * piece)
    share = piece // CUT
    some = len(part) * share
    strips = [
        pl.BlockSpec((share, cols), lambda i, p, n=CUT * core + t: (2 * CUT * i + n, 0)) for core in range(2) for t in part
    ]
    whole = pl.BlockSpec((piece, width), lambda i, p: (0, 0), pipeline_mode=pl.Buffered(1))
    out = pl.BlockSpec((1, some, width), lambda i, p: (i, 0, 0))
    return pl.pallas_call(
        functools.partial(product_kernel, count=len(strips)),
        grid_spec=pltpu.PrefetchScalarGridSpec(
            num_scalar_prefetch=1,
            grid=(blocks,),
            in_specs=[*strips] + [whole] * 8 + [pl.BlockSpec((1, 8, 128), lambda i, p: (0, 0, 0))] * len(after),
            out_specs=[out, out],
            scratch_shapes=[pltpu.VMEM((cols, width), BF)] * 2,
        ),
        out_shape=[jax.ShapeDtypeStruct((blocks, some, width), F32)] * 2,
        compiler_params=pltpu.CompilerParams(vmem_limit_bytes=40 << 20),
        cost_estimate=pl.CostEstimate(
            flops=12 * blocks * some * cols * width,
            bytes_accessed=8 * blocks * some * (cols + width) + 4 * cols * width,
            transcendentals=0,
        ),
    )(places, *[a] * len(strips), *pieces, *after)


def update_kernel(one_ref, two_ref, x_ref, first_ref, second_ref):
    @pl.when(pl.program_id(0) == 0)
    def _():
        first_ref[...] = jnp.zeros_like(first_ref)
        second_ref[...] = jnp.zeros_like(second_ref)

    both, x = jnp.concatenate([one_ref[0], two_ref[0]], axis=0), x_ref[0]
    wide = first_ref.shape[0]
    first_ref[...] += dot3(x[:, :wide], both[:, :wide], ((0,), (0,)))
    second_ref[...] += dot3(x[:, wide:], both[:, wide:], ((0,), (0,)))


def updates(summed, x):
    blocks, piece, width = x.shape
    wide = width // NS
    specs = [pl.BlockSpec((1, *v.shape[1:]), lambda i: (i, 0, 0)) for v in (*summed, x)]
    update = pl.BlockSpec((wide, wide), lambda i: (0, 0))
    return pl.pallas_call(
        update_kernel,
        grid=(blocks,),
        in_specs=specs,
        out_specs=[update, update],
        out_shape=[jax.ShapeDtypeStruct((wide, wide), F32)] * 2,
        compiler_params=pltpu.CompilerParams(vmem_limit_bytes=16 << 20),
        cost_estimate=pl.CostEstimate(
            flops=6 * blocks * piece * width * wide, bytes_accessed=8 * blocks * piece * width, transcendentals=0
        ),
    )(*summed, x)


def gather_column(mine):
    pair = swap(mine, "xh")
    one, three = (lambda i: i ^ 1), (lambda i: i ^ 3)
    mine1 = send(mine, "y", 4, one)
    mine3 = send(mine, "y", 4, three)
    pair3 = send(pair, "y", 4, three)
    mine2 = send(mine1, "y", 4, three)
    pair1 = send(pair, "y", 4, one)
    pair2 = send(pair3, "y", 4, one)
    return [mine, pair, mine1, pair1, mine2, pair2, mine3, pair3]


def local(ancestor_inverse, lower_panel, diag_factor, diag_block, pattern):
    y, xh, z, xl, k = (lax.axis_index(a) for a in ALL)
    row, col = y * 2 + xh, z * 4 + xl * 2 + k
    piece, wide = lower_panel.shape[1:]
    start = (row * 16 + col) * piece
    masks = [tile_mask(pattern, s, start, piece) for s in range(NS)]
    normed = jnp.concatenate(
        [jnp.dot(lower_panel[s], diag_factor[s], precision=HIGHEST) * masks[s] for s in range(NS)], axis=1
    )
    spots = jnp.arange(8, dtype=jnp.int32)
    places = jnp.concatenate([((spots // 2) ^ y) * 2 + ((spots % 2) ^ xh), k[None]])
    mine = lax.ppermute(normed, ALL, transpose_pairs())

    (sent,) = later([normed], [mine])
    band = lax.all_gather(sent, ("z", "xl"), axis=0, tiled=False)

    pieces = gather_column(mine)
    summed = []
    for part in PARTS:
        keep, give = product(ancestor_inverse, pieces, places, part, summed)
        summed.append(keep + swap(give, "k"))
    first, second = updates(summed, band)
    whole = []
    for one in summed:
        over_z = lax.psum_scatter(one.reshape(4, 2, *one.shape[1:]), "z", scatter_dimension=0, tiled=False)
        kept = lax.dynamic_slice_in_dim(over_z, xl, 1, 0)[0]
        taken = swap(lax.dynamic_slice_in_dim(over_z, 1 - xl, 1, 0)[0], "xl")
        whole.append(kept + taken)
    whole = jnp.concatenate(whole, axis=0)
    panels = [-masks[s] * whole[:, s * wide : (s + 1) * wide] for s in range(NS)]
    first, second = total(first, second, taken)
    return jnp.stack(panels), jnp.stack([diag_block[0] + first, diag_block[1] + second])


def solution(mesh):
    fine = Mesh(mesh.devices.reshape(4, 2, 4, 2, 2), ALL)
    rows, cols = ("y", "xh"), ("z", "xl", "k")
    return jax.shard_map(
        local,
        mesh=fine,
        in_specs=(P(rows, cols), P(None, ALL, None), P(), P(), P()),
        out_specs=(P(None, ALL, None), P()),
        check_vma=False,
    )
```

```python
import jax
import jax.numpy as jnp
from jax import lax
from jax.experimental import pallas as pl
from jax.experimental.pallas import tpu as pltpu
from jax.sharding import Mesh, PartitionSpec as P

BS = 64
NS = 2
HIGH = lax.Precision.HIGH
HIGHEST = lax.Precision.HIGHEST
ALL = ("y", "xh", "z", "xl", "k")
BF = jnp.bfloat16
F32 = jnp.float32


def send(x, axis, size, to):
    return lax.ppermute(x, axis, [(i, to(i)) for i in range(size)])


def swap(x, axis):
    return send(x, axis, 2, lambda i: i ^ 1)


def transpose_pairs():
    return [(8 * c + r, 16 * r + c) for r in range(8) for c in range(16)]


def tile_mask(pattern, snode, start, length):
    tiles = lax.dynamic_slice_in_dim(pattern[snode], start // BS, length // BS, 0)
    return jnp.repeat(tiles, BS).astype(F32)[:, None]


def scatter_four(x, axis):
    me = lax.axis_index(axis)
    rows = x.shape[0] // 4
    part = lambda i: lax.dynamic_slice_in_dim(x, lax.rem(i, 4) * rows, rows, 0)
    got = [send(part(me + d), axis, 4, lambda i, d=d: (i + d) % 4) for d in (1, 2, 3)]
    return part(me) + got[0] + got[1] + got[2]


def others_four(x, axis):
    return [send(x, axis, 4, lambda i, d=d: (i + d) % 4) for d in (1, 2, 3)]


def sum_four(x, axis):
    got = others_four(x, axis)
    return x + got[0] + got[1] + got[2]


def gather_four(x, axis):
    me = lax.axis_index(axis)
    one, two, three = others_four(x, axis)
    twice = jnp.concatenate([three, two, one, x, three, two, one], axis=0)
    return lax.dynamic_slice_in_dim(twice, (3 - me) * x.shape[0], 4 * x.shape[0], 0)


def total(first, second, before):
    k = lax.axis_index("k")
    mine = jnp.where(k == 0, first, second) + swap(jnp.where(k == 0, second, first), "k")
    mine = scatter_four(mine, "y")
    mine = sum_four(mine, "z")
    mine = mine + swap(mine, "xl")
    mine = mine + swap(mine, "xh")
    mine = gather_four(mine, "y")
    (mine,) = later([mine], [before])
    other = swap(mine, "k")
    return jnp.where(k == 0, mine, other), jnp.where(k == 0, other, mine)


def halves(x):
    high = x.astype(BF)
    return high, (x - high.astype(F32)).astype(BF)


def dot3(a, b, dims):
    ah, al = halves(a)
    bh, bl = halves(b)
    f = lambda p, q: lax.dot_general(p, q, (dims, ((), ())), preferred_element_type=F32)
    return f(ah, bh) + (f(ah, bl) + f(al, bh))


def later(xs, after):
    anywhere = pl.BlockSpec(memory_space=pl.ANY)
    return pl.pallas_call(
        lambda *refs: None,
        in_specs=[anywhere] * (len(xs) + len(after)),
        out_specs=[anywhere] * len(xs),
        out_shape=[jax.ShapeDtypeStruct(x.shape, x.dtype) for x in xs],
        input_output_aliases={i: i for i in range(len(xs))},
        cost_estimate=pl.CostEstimate(flops=0, bytes_accessed=0, transcendentals=0),
    )(*xs, *after)


def normed_kernel(panel_ref, factor_ref, mask_ref, out_ref):
    wide = factor_ref.shape[-1]
    for s in range(NS):
        rows = jnp.dot(panel_ref[s], factor_ref[s], precision=HIGHEST, preferred_element_type=F32)
        out_ref[:, s * wide : (s + 1) * wide] = rows * mask_ref[s]


def normed_rows(panel, factor, masks):
    count, piece, wide = panel.shape
    return pl.pallas_call(
        normed_kernel,
        out_shape=jax.ShapeDtypeStruct((piece, count * wide), F32),
        compiler_params=pltpu.CompilerParams(vmem_limit_bytes=16 << 20),
        cost_estimate=pl.CostEstimate(
            flops=12 * count * piece * wide * wide, bytes_accessed=8 * count * piece * wide, transcendentals=0
        ),
    )(panel, factor, masks)


def product_kernel(place_ref, a_ref, *refs):
    pieces, (keep_ref, give_ref, high, low) = refs[:8], refs[8:]
    piece = pieces[0].shape[0]

    @pl.when(pl.program_id(0) == 0)
    def _():
        for j in range(8):
            rows = pl.ds(pl.multiple_of(place_ref[j] * piece, BS), piece)
            xh, xl = halves(pieces[j][...])
            high[rows, :] = xh
            low[rows, :] = xl

    ah, al = halves(a_ref[...])
    f = lambda p, q: jnp.dot(p, q, preferred_element_type=F32)
    out = f(ah, high[...]) + (f(ah, low[...]) + f(al, high[...]))
    first, second = out[:piece], out[piece:]
    lower = place_ref[8] == 0
    keep_ref[0] = jnp.where(lower, first, second)
    give_ref[0] = jnp.where(lower, second, first)


def product(a, pieces, places, part):
    rows, cols = a.shape[0] // 2, a.shape[1]
    piece, width = pieces[0].shape
    blocks = rows // (2 * piece)
    whole = pl.BlockSpec((piece, width), lambda i, p: (0, 0), pipeline_mode=pl.Buffered(1))
    out = pl.BlockSpec((1, piece, width), lambda i, p: (i, 0, 0))
    return pl.pallas_call(
        product_kernel,
        grid_spec=pltpu.PrefetchScalarGridSpec(
            num_scalar_prefetch=1,
            grid=(blocks,),
            in_specs=[pl.BlockSpec((2 * piece, cols), lambda i, p: (2 * i + part, 0))] + [whole] * 8,
            out_specs=[out, out],
            scratch_shapes=[pltpu.VMEM((cols, width), BF)] * 2,
        ),
        out_shape=[jax.ShapeDtypeStruct((blocks, piece, width), F32)] * 2,
        compiler_params=pltpu.CompilerParams(vmem_limit_bytes=40 << 20),
        cost_estimate=pl.CostEstimate(
            flops=6 * rows * cols * width, bytes_accessed=4 * (rows * cols + (rows + cols) * width), transcendentals=0
        ),
    )(places, a, *pieces)


def update_kernel(near_ref, far_ref, x_ref, first_ref, second_ref):
    @pl.when(pl.program_id(0) == 0)
    def _():
        first_ref[...] = jnp.zeros_like(first_ref)
        second_ref[...] = jnp.zeros_like(second_ref)

    wide = first_ref.shape[0]
    for h, ref in enumerate((near_ref, far_ref)):
        both, x = ref[0], x_ref[h]
        first_ref[...] += dot3(x[:, :wide], both[:, :wide], ((0,), (0,)))
        second_ref[...] += dot3(x[:, wide:], both[:, wide:], ((0,), (0,)))


def updates(halved, x):
    blocks, piece, width = halved[0].shape
    wide = width // NS
    spec = pl.BlockSpec((1, piece, width), lambda i: (i, 0, 0))
    update = pl.BlockSpec((wide, wide), lambda i: (0, 0))
    return pl.pallas_call(
        update_kernel,
        grid=(blocks,),
        in_specs=[spec, spec, pl.BlockSpec((2, piece, width), lambda i: (i, 0, 0))],
        out_specs=[update, update],
        out_shape=[jax.ShapeDtypeStruct((wide, wide), F32)] * 2,
        compiler_params=pltpu.CompilerParams(vmem_limit_bytes=16 << 20),
        cost_estimate=pl.CostEstimate(
            flops=12 * blocks * piece * width * wide, bytes_accessed=16 * blocks * piece * width, transcendentals=0
        ),
    )(*halved, x)


def gather_column(mine):
    pair = swap(mine, "xh")
    one, three = (lambda i: i ^ 1), (lambda i: i ^ 3)
    mine1 = send(mine, "y", 4, one)
    mine3 = send(mine, "y", 4, three)
    pair3 = send(pair, "y", 4, three)
    mine2 = send(mine1, "y", 4, three)
    pair1 = send(pair, "y", 4, one)
    pair2 = send(pair3, "y", 4, one)
    return [mine, pair, mine1, pair1, mine2, pair2, mine3, pair3]


def local(ancestor_inverse, lower_panel, diag_factor, diag_block, pattern):
    y, xh, z, xl, k = (lax.axis_index(a) for a in ALL)
    row, col = y * 2 + xh, z * 4 + xl * 2 + k
    piece, wide = lower_panel.shape[1:]
    start = (row * 16 + col) * piece
    masks = [tile_mask(pattern, s, start, piece) for s in range(NS)]
    normed = normed_rows(lower_panel, diag_factor, jnp.stack(masks))
    spots = jnp.arange(8, dtype=jnp.int32)
    places = jnp.concatenate([((spots // 2) ^ y) * 2 + ((spots % 2) ^ xh), k[None]])
    mine = lax.ppermute(normed, ALL, transpose_pairs())

    (sent,) = later([normed], [mine])
    band = lax.all_gather(sent, ("z", "xl"), axis=0, tiled=False)

    pieces = gather_column(mine)
    halved = []
    for part in range(2):
        keep, give = product(ancestor_inverse, pieces, places, part)
        halved.append(keep + swap(give, "k"))
    first, second = updates(halved, band)
    sums = [lax.psum_scatter(h, "z", scatter_dimension=0, tiled=False) for h in halved]
    given = jnp.where(xl == 0, sums[1], sums[0])
    taken = swap(given, "xl")
    whole = jnp.where(xl == 0, sums[0], sums[1]) + taken
    panels = [-masks[s] * whole[:, s * wide : (s + 1) * wide] for s in range(NS)]
    first, second = total(first, second, taken)
    return jnp.stack(panels), jnp.stack([diag_block[0] + first, diag_block[1] + second])


def solution(mesh):
    fine = Mesh(mesh.devices.reshape(4, 2, 4, 2, 2), ALL)
    rows, cols = ("y", "xh"), ("z", "xl", "k")
    return jax.shard_map(
        local,
        mesh=fine,
        in_specs=(P(rows, cols), P(None, ALL, None), P(), P(), P()),
        out_specs=(P(None, ALL, None), P()),
        check_vma=False,
    )
```

```python
import jax
import jax.numpy as jnp
from jax import lax
from jax.experimental import pallas as pl
from jax.experimental.pallas import tpu as pltpu
from jax.sharding import Mesh, PartitionSpec as P

BS = 64
NS = 2
HIGH = lax.Precision.HIGH
HIGHEST = lax.Precision.HIGHEST
ALL = ("y", "xh", "z", "xl", "k")
BF = jnp.bfloat16
F32 = jnp.float32


def send(x, axis, size, to):
    return lax.ppermute(x, axis, [(i, to(i)) for i in range(size)])


def swap(x, axis):
    return send(x, axis, 2, lambda i: i ^ 1)


def transpose_pairs():
    return [(8 * c + r, 16 * r + c) for r in range(8) for c in range(16)]


def tile_mask(pattern, snode, start, length):
    tiles = lax.dynamic_slice_in_dim(pattern[snode], start // BS, length // BS, 0)
    return jnp.repeat(tiles, BS).astype(F32)[:, None]


def scatter_four(x, axis):
    me = lax.axis_index(axis)
    rows = x.shape[0] // 4
    part = lambda i: lax.dynamic_slice_in_dim(x, lax.rem(i, 4) * rows, rows, 0)
    got = [send(part(me + d), axis, 4, lambda i, d=d: (i + d) % 4) for d in (1, 2, 3)]
    return part(me) + got[0] + got[1] + got[2]


def others_four(x, axis):
    return [send(x, axis, 4, lambda i, d=d: (i + d) % 4) for d in (1, 2, 3)]


def sum_four(x, axis):
    got = others_four(x, axis)
    return x + got[0] + got[1] + got[2]


def gather_four(x, axis):
    me = lax.axis_index(axis)
    one, two, three = others_four(x, axis)
    twice = jnp.concatenate([three, two, one, x, three, two, one], axis=0)
    return lax.dynamic_slice_in_dim(twice, (3 - me) * x.shape[0], 4 * x.shape[0], 0)


def total(first, second, before):
    k = lax.axis_index("k")
    mine = jnp.where(k == 0, first, second) + swap(jnp.where(k == 0, second, first), "k")
    mine = scatter_four(mine, "y")
    mine = sum_four(mine, "z")
    mine = mine + swap(mine, "xl")
    mine = mine + swap(mine, "xh")
    mine = gather_four(mine, "y")
    (mine,) = later([mine], [before])
    other = swap(mine, "k")
    return jnp.where(k == 0, mine, other), jnp.where(k == 0, other, mine)


def halves(x):
    high = x.astype(BF)
    return high, (x - high.astype(F32)).astype(BF)


def dot3(a, b, dims):
    ah, al = halves(a)
    bh, bl = halves(b)
    f = lambda p, q: lax.dot_general(p, q, (dims, ((), ())), preferred_element_type=F32)
    return f(ah, bh) + (f(ah, bl) + f(al, bh))


def later(xs, after):
    anywhere = pl.BlockSpec(memory_space=pl.ANY)
    return pl.pallas_call(
        lambda *refs: None,
        in_specs=[anywhere] * (len(xs) + len(after)),
        out_specs=[anywhere] * len(xs),
        out_shape=[jax.ShapeDtypeStruct(x.shape, x.dtype) for x in xs],
        input_output_aliases={i: i for i in range(len(xs))},
        cost_estimate=pl.CostEstimate(flops=0, bytes_accessed=0, transcendentals=0),
    )(*xs, *after)


def normed_kernel(panel_ref, factor_ref, mask_ref, out_ref):
    wide = factor_ref.shape[-1]
    for s in range(NS):
        rows = jnp.dot(panel_ref[s], factor_ref[s], precision=HIGHEST, preferred_element_type=F32)
        out_ref[:, s * wide : (s + 1) * wide] = rows * mask_ref[s]


def normed_rows(panel, factor, masks):
    count, piece, wide = panel.shape
    return pl.pallas_call(
        normed_kernel,
        out_shape=jax.ShapeDtypeStruct((piece, count * wide), F32),
        compiler_params=pltpu.CompilerParams(vmem_limit_bytes=56 << 20),
        cost_estimate=pl.CostEstimate(
            flops=12 * count * piece * wide * wide, bytes_accessed=8 * count * piece * wide, transcendentals=0
        ),
    )(panel, factor, masks)


def product_kernel(place_ref, a_ref, *refs):
    pieces, (keep_ref, give_ref, high, low) = refs[:8], refs[8:]
    piece = pieces[0].shape[0]

    @pl.when(pl.program_id(0) == 0)
    def _():
        for j in range(8):
            rows = pl.ds(pl.multiple_of(place_ref[j] * piece, BS), piece)
            xh, xl = halves(pieces[j][...])
            high[rows, :] = xh
            low[rows, :] = xl

    ah, al = halves(a_ref[...])
    f = lambda p, q: jnp.dot(p, q, preferred_element_type=F32)
    out = f(ah, high[...]) + (f(ah, low[...]) + f(al, high[...]))
    first, second = out[:piece], out[piece:]
    lower = place_ref[8] == 0
    keep_ref[0] = jnp.where(lower, first, second)
    give_ref[0] = jnp.where(lower, second, first)


def product(a, pieces, places, part):
    rows, cols = a.shape[0] // 2, a.shape[1]
    piece, width = pieces[0].shape
    blocks = rows // (2 * piece)
    whole = pl.BlockSpec((piece, width), lambda i, p: (0, 0), pipeline_mode=pl.Buffered(1))
    out = pl.BlockSpec((1, piece, width), lambda i, p: (i, 0, 0))
    return pl.pallas_call(
        product_kernel,
        grid_spec=pltpu.PrefetchScalarGridSpec(
            num_scalar_prefetch=1,
            grid=(blocks,),
            in_specs=[pl.BlockSpec((2 * piece, cols), lambda i, p: (2 * i + part, 0))] + [whole] * 8,
            out_specs=[out, out],
            scratch_shapes=[pltpu.VMEM((cols, width), BF)] * 2,
        ),
        out_shape=[jax.ShapeDtypeStruct((blocks, piece, width), F32)] * 2,
        compiler_params=pltpu.CompilerParams(vmem_limit_bytes=40 << 20),
        cost_estimate=pl.CostEstimate(
            flops=6 * rows * cols * width, bytes_accessed=4 * (rows * cols + (rows + cols) * width), transcendentals=0
        ),
    )(places, a, *pieces)


def update_kernel(near_ref, far_ref, x_ref, first_ref, second_ref):
    @pl.when(pl.program_id(0) == 0)
    def _():
        first_ref[...] = jnp.zeros_like(first_ref)
        second_ref[...] = jnp.zeros_like(second_ref)

    wide = first_ref.shape[0]
    for h, ref in enumerate((near_ref, far_ref)):
        both, x = ref[0], x_ref[h]
        first_ref[...] += dot3(x[:, :wide], both[:, :wide], ((0,), (0,)))
        second_ref[...] += dot3(x[:, wide:], both[:, wide:], ((0,), (0,)))


def updates(halved, x):
    blocks, piece, width = halved[0].shape
    wide = width // NS
    spec = pl.BlockSpec((1, piece, width), lambda i: (i, 0, 0))
    update = pl.BlockSpec((wide, wide), lambda i: (0, 0))
    return pl.pallas_call(
        update_kernel,
        grid=(blocks,),
        in_specs=[spec, spec, pl.BlockSpec((2, piece, width), lambda i: (i, 0, 0))],
        out_specs=[update, update],
        out_shape=[jax.ShapeDtypeStruct((wide, wide), F32)] * 2,
        compiler_params=pltpu.CompilerParams(vmem_limit_bytes=16 << 20),
        cost_estimate=pl.CostEstimate(
            flops=12 * blocks * piece * width * wide, bytes_accessed=16 * blocks * piece * width, transcendentals=0
        ),
    )(*halved, x)


def gather_column(mine):
    pair = swap(mine, "xh")
    one, three = (lambda i: i ^ 1), (lambda i: i ^ 3)
    mine1 = send(mine, "y", 4, one)
    mine3 = send(mine, "y", 4, three)
    pair3 = send(pair, "y", 4, three)
    mine2 = send(mine1, "y", 4, three)
    pair1 = send(pair, "y", 4, one)
    pair2 = send(pair3, "y", 4, one)
    return [mine, pair, mine1, pair1, mine2, pair2, mine3, pair3]


def local(ancestor_inverse, lower_panel, diag_factor, diag_block, pattern):
    y, xh, z, xl, k = (lax.axis_index(a) for a in ALL)
    row, col = y * 2 + xh, z * 4 + xl * 2 + k
    piece, wide = lower_panel.shape[1:]
    start = (row * 16 + col) * piece
    masks = [tile_mask(pattern, s, start, piece) for s in range(NS)]
    normed = normed_rows(lower_panel, diag_factor, jnp.stack(masks))
    spots = jnp.arange(8, dtype=jnp.int32)
    places = jnp.concatenate([((spots // 2) ^ y) * 2 + ((spots % 2) ^ xh), k[None]])
    mine = lax.ppermute(normed, ALL, transpose_pairs())

    (sent,) = later([normed], [mine])
    band = lax.all_gather(sent, ("z", "xl"), axis=0, tiled=False)

    pieces = gather_column(mine)
    halved = []
    for part in range(2):
        keep, give = product(ancestor_inverse, pieces, places, part)
        halved.append(keep + swap(give, "k"))
    first, second = updates(halved, band)
    sums = [lax.psum_scatter(h, "z", scatter_dimension=0, tiled=False) for h in halved]
    given = jnp.where(xl == 0, sums[1], sums[0])
    taken = swap(given, "xl")
    whole = jnp.where(xl == 0, sums[0], sums[1]) + taken
    panels = [-masks[s] * whole[:, s * wide : (s + 1) * wide] for s in range(NS)]
    first, second = total(first, second, taken)
    return jnp.stack(panels), jnp.stack([diag_block[0] + first, diag_block[1] + second])


def solution(mesh):
    fine = Mesh(mesh.devices.reshape(4, 2, 4, 2, 2), ALL)
    rows, cols = ("y", "xh"), ("z", "xl", "k")
    return jax.shard_map(
        local,
        mesh=fine,
        in_specs=(P(rows, cols), P(None, ALL, None), P(), P(), P()),
        out_specs=(P(None, ALL, None), P()),
        check_vma=False,
    )
```
